256 devices in a mesh: dp: 32 (over z, x), cent: 8 (over y, core).
Axes of the slice: x: 4, y: 4, z: 8, core: 2. Of those that a mesh axis runs over, the one named last changes fastest.
Arguments:
- embeddings: bfloat16 [32768, 768], P('dp'), may hold values from -2 to 2
- centroids: float32 [8192, 768], P(('dp', 'cent')), may hold values from -1 to 1
Outputs:
- new_centroids: float32 [8192, 768], P(('dp', 'cent'))
- counts: float32 [8192], P(('dp', 'cent'))
- row_lse: float32 [32768], P('dp')
The draws below stay inside these ranges and needn't reach their ends.
All inputs are finite; a program needn't handle non-finite values.
Results may differ from the reference program's by a relative error of at most 0.02.
Values may be sent and summed in bfloat16 or wider, within the bound.
No kernel may reach another device: no remote copies, remote signals or barrier semaphores. Data moves between devices by JAX's collectives and lax.ppermute only.
A program may use at most 64 MiB of HBM per device.

```python
import jax
import jax.numpy as jnp
from jax import lax

D = 768
ITERS = 2
ROWS = 32768
CENTS = 8192
BLOCK = 1024


def base_centers(key):
    return jax.random.normal(jax.random.fold_in(key, 11), (CENTS, D), jnp.float32) * D ** (-0.5)


def draw_centroids(key, part):
    centers = base_centers(key)
    return jnp.clip(centers, -1.0, 1.0)


def draw_embeddings(key, part):
    key = jax.random.fold_in(key, 2)
    rows = jax.random.normal(key, (ROWS, D), jnp.float32) * D ** (-0.5)
    return jnp.clip(rows, -2.0, 2.0).astype(jnp.bfloat16)


def setup_inputs(seed: int = 0) -> dict:
    keys = jax.random.split(jax.random.key(seed), 3)
    return {
        "embeddings": draw_embeddings(jax.random.fold_in(keys[2], 71), 0),
        "centroids": draw_centroids(jax.random.fold_in(keys[2], 71), 0),
    }


sharpness = 50.0


def reference(embeddings, centroids):
    current = centroids
    counts = jnp.zeros((CENTS,), jnp.float32)
    row_lse = jnp.zeros((ROWS,), jnp.float32)
    blocks = embeddings.reshape(ROWS // BLOCK, BLOCK, D)
    for step in range(ITERS):
        copy = current.astype(jnp.bfloat16)
        squares = jnp.sum(jnp.square(copy.astype(jnp.float32)), axis=1)

        def one_block(carry, rows):
            sums, weights = carry
            logits = (jnp.dot(rows, copy.T, preferred_element_type=jnp.float32) - 0.5 * squares) * sharpness
            peak = jnp.max(logits, axis=1)
            total = jnp.sum(jnp.exp(logits - peak[:, None]), axis=1)
            log_total = peak + jnp.log(total)
            resp = jnp.exp(logits - log_total[:, None]).astype(jnp.bfloat16)
            sums = sums + jnp.dot(resp.T, rows, preferred_element_type=jnp.float32)
            weights = weights + jnp.sum(resp.astype(jnp.float32), axis=0)
            return (sums, weights), log_total

        start = (jnp.zeros((CENTS, D), jnp.float32), jnp.zeros((CENTS,), jnp.float32))
        (sums, counts), parts = lax.scan(one_block, start, blocks)
        row_lse = parts.reshape(ROWS)
        current = (sums + current) / (counts[:, None] + 1.0)
    return current, counts, row_lse
```

```python
import functools
import math

import jax
import jax.numpy as jnp
from jax import lax
from jax.experimental import pallas as pl
from jax.experimental.pallas import tpu as pltpu
from jax.sharding import Mesh
from jax.sharding import PartitionSpec as P

ITERS = 2
D = 768
Z, X, Y, C = 8, 4, 4, 2
OWN = 32
K = Z * OWN
COL = 1024
HALF = COL // 2
CHUNK = 512
WIDE = D + 128
F32, BF16 = jnp.float32, jnp.bfloat16
SCALE = 50.0 * math.log2(math.e)
VMEM = pl.BlockSpec(memory_space=pltpu.VMEM)
ANY = pl.BlockSpec(memory_space=pl.ANY)
SMEM = pl.BlockSpec(memory_space=pltpu.SMEM)


def rows_to_tile(v):
    return jnp.concatenate([v[:, i * 128 : (i + 1) * 128] for i in range(v.shape[1] // 128)], axis=0)


def tile_to_rows(v):
    return jnp.concatenate([v[i : i + 1] for i in range(v.shape[0])], axis=1)


def swap_halves(v, c):
    h = v.shape[0] // 2
    return jnp.where(c == 0, v, jnp.concatenate([v[h:], v[:h]], axis=0))


def load_all(pieces, emb, sems):
    waits, at = [], 0
    for piece in pieces:
        for i in range(piece.shape[0] // CHUNK):
            copy = pltpu.make_async_copy(
                piece.at[pl.ds(i * CHUNK, CHUNK)], emb.at[pl.ds(at, CHUNK)], sems.at[len(waits)]
            )
            copy.start()
            waits.append(copy)
            at += CHUNK
    return waits


def score_kernel(n, first, merge, *refs):
    idx, cent_ref = refs[:2]
    refs = refs[2:]
    if merge:
        own_ref, refs = refs[0], refs[1:]
    pieces, (p_ref, m_ref, l_ref, emb, sems) = refs[:n], refs[n:]
    waits = load_all(pieces, emb, sems)
    cent = cent_ref[...]
    wide = cent.astype(F32)
    half_squares = (0.5 * SCALE) * jnp.sum(wide * wide, axis=1, keepdims=True)
    x, c = idx[0], idx[1]
    lse = []
    for i, wait in enumerate(waits):
        wait.wait()
        rows = pl.ds(i * CHUNK, CHUNK)
        dots = lax.dot_general(
            cent, emb[rows, :], (((1,), (1,)), ((), ())), preferred_element_type=F32
        )
        logits = dots * SCALE - half_squares
        peak = jnp.max(logits, axis=0, keepdims=True)
        p = jnp.exp2(logits - peak)
        total = jnp.sum(p, axis=0, keepdims=True)
        p_ref[:, rows] = p.astype(BF16)
        m_ref[pl.ds(i * 4, 4), :] = rows_to_tile(peak)
        lse.append(rows_to_tile(peak + jnp.log2(total)))
    if merge:
        l_ref[pl.ds(8 * x, 8), :] = own_ref[...]
    for j in range(len(lse) // 2):
        column = jnp.concatenate(lse[2 * j : 2 * j + 2], axis=0)
        k = first + j
        if k == 0:
            if l_ref.shape[0] == 8:
                l_ref[...] = column
            else:
                l_ref[pl.ds(8 * x, 8), :] = column
        else:
            l_ref[pl.ds(8 * lax.rem(x + (X - k), X), 8), :] = swap_halves(column, c)


def score(idx, cent, pieces, first, own=None):
    rows = sum(p.shape[0] for p in pieces)
    out = 8 if (first == 0 and rows == COL) else X * 8
    merge = own is not None
    return pl.pallas_call(
        functools.partial(score_kernel, len(pieces), first, merge),
        out_shape=(
            jax.ShapeDtypeStruct((K, rows), BF16),
            jax.ShapeDtypeStruct((rows // 128, 128), F32),
            jax.ShapeDtypeStruct((out, 128), F32),
        ),
        in_specs=[SMEM, VMEM] + [VMEM] * merge + [ANY] * len(pieces),
        out_specs=(VMEM, VMEM, VMEM),
        scratch_shapes=[
            pltpu.VMEM((rows, D), BF16),
            pltpu.SemaphoreType.DMA((rows // CHUNK,)),
        ],
        compiler_params=pltpu.CompilerParams(vmem_limit_bytes=24 << 20),
        name="score",
    )(idx, cent, *([own] if merge else []), *pieces)


def sum_kernel(n, np_, *refs):
    idx, parts_ref = refs[:2]
    refs = refs[2:]
    ps, ms, pieces = refs[:np_], refs[np_ : 2 * np_], refs[2 * np_ : 2 * np_ + n]
    out_ref, lse_ref, emb, sems = refs[2 * np_ + n :]
    waits = load_all(pieces, emb, sems)
    x, c = idx[0], idx[1]
    parts = [parts_ref[pl.ds(i * 32, 32), :] for i in range(X * Y)]
    peak = functools.reduce(jnp.maximum, parts)
    total = sum(jnp.exp2(v - peak) for v in parts)
    lse_ref[...] = peak + jnp.log2(total)
    acc = jnp.zeros((K, D), F32)
    weights = jnp.zeros((K, 128), F32)
    at = 0
    for p_ref, m_ref in zip(ps, ms):
        for j in range(p_ref.shape[1] // COL):
            k = at // 2
            lse = lse_ref[pl.ds(8 * lax.rem(x + (X - k), X), 8), :]
            if k > 0:
                lse = swap_halves(lse, c)
            factor = jnp.exp2(m_ref[pl.ds(j * 8, 8), :] - lse)
            for h in range(2):
                f = tile_to_rows(factor[4 * h : 4 * h + 4])
                p = p_ref[:, pl.ds((2 * j + h) * CHUNK, CHUNK)].astype(F32)
                resp = (p * f).astype(BF16)
                waits[at].wait()
                acc += jnp.dot(resp, emb[pl.ds(at * CHUNK, CHUNK), :], preferred_element_type=F32)
                wide = resp.astype(F32)
                for i in range(CHUNK // 128):
                    weights += wide[:, i * 128 : (i + 1) * 128]
                at += 1
    counts = jnp.sum(weights, axis=1, keepdims=True)
    high = counts.astype(BF16).astype(F32)
    lane = lax.broadcasted_iota(jnp.int32, (K, 128), 1)
    tail = jnp.where(lane == 0, high, jnp.where(lane == 1, counts - high, 0.0))
    out_ref[:, :D] = acc.astype(BF16)
    out_ref[:, D:] = tail.astype(BF16)


def sums_of(idx, parts, ps, ms, pieces):
    rows = X * COL
    return pl.pallas_call(
        functools.partial(sum_kernel, len(pieces), len(ps)),
        out_shape=(
            jax.ShapeDtypeStruct((K, WIDE), BF16),
            jax.ShapeDtypeStruct((X * 8, 128), F32),
        ),
        in_specs=[SMEM, VMEM] + [VMEM] * (2 * len(ps)) + [ANY] * len(pieces),
        out_specs=(VMEM, VMEM),
        scratch_shapes=[
            pltpu.VMEM((rows, D), BF16),
            pltpu.SemaphoreType.DMA((rows // CHUNK,)),
        ],
        compiler_params=pltpu.CompilerParams(vmem_limit_bytes=24 << 20),
        name="sums",
    )(idx, parts, *ps, *ms, *pieces)


def update_kernel(got_ref, cur_ref, new_ref, copies_ref, counts_ref):
    total = got_ref[pl.ds(0, OWN), :].astype(F32)
    for i in range(1, Z):
        total += got_ref[pl.ds(i * OWN, OWN), :].astype(F32)
    counts = total[:, D : D + 1] + total[:, D + 1 : D + 2]
    new = (total[:, :D] + cur_ref[...]) / (counts + 1.0)
    new_ref[...] = new
    for i in range(Z):
        copies_ref[pl.ds(i * OWN, OWN), :] = new.astype(BF16)
    counts_ref[...] = jnp.broadcast_to(counts, (OWN, 128))


def update(got, current):
    return pl.pallas_call(
        update_kernel,
        out_shape=(
            jax.ShapeDtypeStruct((OWN, D), F32),
            jax.ShapeDtypeStruct((K, D), BF16),
            jax.ShapeDtypeStruct((OWN, 128), F32),
        ),
        in_specs=[VMEM, VMEM],
        out_specs=(VMEM, VMEM, VMEM),
        name="update",
    )(got, current)


def shift(v, axis, size, k):
    return lax.ppermute(v, axis, [(i, (i + k) % size) for i in range(size)])


def on_device(embeddings, centroids):
    x, c = lax.axis_index("x"), lax.axis_index("c")
    idx = jnp.stack([x, c]).astype(jnp.int32)
    mine = lax.dynamic_slice_in_dim(embeddings, c * HALF, HALF, 0)
    near = {k: shift(mine, "x", X, k) for k in (1, 3, 2)}
    pieces = [embeddings]
    for k in (1, 2, 3):
        pieces += [near[k], shift(near[k], "c", C, 1)]
    copies = jnp.tile(centroids.astype(BF16), (Z, 1))
    current = centroids
    for step in range(ITERS):
        cent = lax.all_to_all(copies, "z", 0, 0, tiled=True)
        if step == 0:
            p0, m0, l0 = score(idx, cent, pieces[:1], 0)
            p1, m1, lse = score(idx, cent, pieces[1:], 1, l0)
            ps, ms = [p0, p1], [m0, m1]
        else:
            p, m, lse = score(idx, cent, pieces, 0)
            ps, ms = [p], [m]
        lse = jnp.logaddexp2(lse, shift(lse, "c", C, 1))
        parts = lax.all_to_all(jnp.tile(lse, (X * Y, 1)), ("x", "y"), 0, 0, tiled=True)
        out, total = sums_of(idx, parts, ps, ms, pieces)
        got = lax.all_to_all(out, "z", 0, 0, tiled=True)
        current, copies, counts = update(got, current)
    row_lse = lax.dynamic_slice_in_dim(total, x * 8, 8, 0).reshape(COL) * math.log(2.0)
    return current, counts[:, 0], row_lse


def solution(mesh):
    split = Mesh(mesh.devices.reshape(Z, X, Y, C), ("z", "x", "y", "c"))
    dp, every = ("z", "x"), ("z", "x", "y", "c")
    return jax.shard_map(
        on_device,
        mesh=split,
        in_specs=(P(dp, None), P(every, None)),
        out_specs=(P(every, None), P(every), P(dp)),
        check_vma=False,
    )
```

```python
import functools
import math

import jax
import jax.numpy as jnp
from jax import lax
from jax.experimental import pallas as pl
from jax.experimental.pallas import tpu as pltpu
from jax.sharding import Mesh
from jax.sharding import PartitionSpec as P

ITERS = 2
D = 768
Z, X, Y, C = 8, 4, 4, 2
OWN = 32
K = Z * OWN
COL = 1024
HALF = COL // 2
CHUNK = 512
WIDE = D + 128
F32, BF16 = jnp.float32, jnp.bfloat16
SCALE = 50.0 * math.log2(math.e)
VMEM = pl.BlockSpec(memory_space=pltpu.VMEM)
ANY = pl.BlockSpec(memory_space=pl.ANY)
SMEM = pl.BlockSpec(memory_space=pltpu.SMEM)


def rows_to_tile(v):
    return jnp.concatenate([v[:, i * 128 : (i + 1) * 128] for i in range(v.shape[1] // 128)], axis=0)


def tile_to_rows(v):
    return jnp.concatenate([v[i : i + 1] for i in range(v.shape[0])], axis=1)


def swap_halves(v, c):
    h = v.shape[0] // 2
    return jnp.where(c == 0, v, jnp.concatenate([v[h:], v[:h]], axis=0))


def load_all(pieces, emb, sems):
    waits, at = [], 0
    for piece in pieces:
        for i in range(piece.shape[0] // CHUNK):
            copy = pltpu.make_async_copy(
                piece.at[pl.ds(i * CHUNK, CHUNK)], emb.at[pl.ds(at, CHUNK)], sems.at[len(waits)]
            )
            copy.start()
            waits.append(copy)
            at += CHUNK
    return waits


def score_kernel(n, first, merge, *refs):
    idx, cent_ref = refs[:2]
    refs = refs[2:]
    if merge:
        own_ref, refs = refs[0], refs[1:]
    pieces, (p_ref, m_ref, l_ref, emb, sems) = refs[:n], refs[n:]
    waits = load_all(pieces, emb, sems)
    cent = cent_ref[...]
    wide = cent.astype(F32)
    half_squares = (0.5 * SCALE) * jnp.sum(wide * wide, axis=1, keepdims=True)
    x, c = idx[0], idx[1]
    lse = []
    step = emb.shape[0] // (1 if emb.shape[0] == COL else 2)
    for at in range(0, emb.shape[0], step):
        for wait in waits[at // CHUNK : (at + step) // CHUNK]:
            wait.wait()
        rows = pl.ds(at, step)
        dots = lax.dot_general(
            cent, emb[rows, :], (((1,), (1,)), ((), ())), preferred_element_type=F32
        )
        logits = dots * SCALE - half_squares
        peak = jnp.max(logits, axis=0, keepdims=True)
        p = jnp.exp2(logits - peak)
        total = jnp.sum(p, axis=0, keepdims=True)
        p_ref[:, rows] = p.astype(BF16)
        m_ref[pl.ds(at // 128, step // 128), :] = rows_to_tile(peak)
        lse.append(rows_to_tile(peak + jnp.log2(total)))
    lse = jnp.concatenate(lse, axis=0)
    if merge:
        l_ref[pl.ds(8 * x, 8), :] = own_ref[...]
    for j in range(emb.shape[0] // COL):
        column = lse[8 * j : 8 * j + 8]
        k = first + j
        if k == 0:
            if l_ref.shape[0] == 8:
                l_ref[...] = column
            else:
                l_ref[pl.ds(8 * x, 8), :] = column
        else:
            l_ref[pl.ds(8 * lax.rem(x + (X - k), X), 8), :] = swap_halves(column, c)


def score(idx, cent, pieces, first, own=None):
    rows = sum(p.shape[0] for p in pieces)
    out = 8 if (first == 0 and rows == COL) else X * 8
    merge = own is not None
    return pl.pallas_call(
        functools.partial(score_kernel, len(pieces), first, merge),
        out_shape=(
            jax.ShapeDtypeStruct((K, rows), BF16),
            jax.ShapeDtypeStruct((rows // 128, 128), F32),
            jax.ShapeDtypeStruct((out, 128), F32),
        ),
        in_specs=[SMEM, VMEM] + [VMEM] * merge + [ANY] * len(pieces),
        out_specs=(VMEM, VMEM, VMEM),
        scratch_shapes=[
            pltpu.VMEM((rows, D), BF16),
            pltpu.SemaphoreType.DMA((rows // CHUNK,)),
        ],
        compiler_params=pltpu.CompilerParams(vmem_limit_bytes=24 << 20),
        name="score",
    )(idx, cent, *([own] if merge else []), *pieces)


def sum_kernel(n, np_, *refs):
    idx, parts_ref = refs[:2]
    refs = refs[2:]
    ps, ms, pieces = refs[:np_], refs[np_ : 2 * np_], refs[2 * np_ : 2 * np_ + n]
    out_ref, lse_ref, emb, sems = refs[2 * np_ + n :]
    waits = load_all(pieces, emb, sems)
    x, c = idx[0], idx[1]
    parts = [parts_ref[pl.ds(i * 32, 32), :] for i in range(X * Y)]
    peak = functools.reduce(jnp.maximum, parts)
    total = sum(jnp.exp2(v - peak) for v in parts)
    lse_ref[...] = peak + jnp.log2(total)
    weights = jnp.zeros((K, 128), F32)
    resps = []
    at = 0
    for p_ref, m_ref in zip(ps, ms):
        for j in range(p_ref.shape[1] // COL):
            k = at // 2
            lse = lse_ref[pl.ds(8 * lax.rem(x + (X - k), X), 8), :]
            if k > 0:
                lse = swap_halves(lse, c)
            factor = jnp.exp2(m_ref[pl.ds(j * 8, 8), :] - lse)
            for h in range(2):
                f = tile_to_rows(factor[4 * h : 4 * h + 4])
                p = p_ref[:, pl.ds((2 * j + h) * CHUNK, CHUNK)].astype(F32)
                resp = (p * f).astype(BF16)
                wide = resp.astype(F32)
                for i in range(CHUNK // 128):
                    weights += wide[:, i * 128 : (i + 1) * 128]
                resps.append(resp)
                at += 1
    for wait in waits:
        wait.wait()
    acc = jnp.dot(jnp.concatenate(resps, axis=1), emb[...], preferred_element_type=F32)
    counts = jnp.sum(weights, axis=1, keepdims=True)
    high = counts.astype(BF16).astype(F32)
    lane = lax.broadcasted_iota(jnp.int32, (K, 128), 1)
    tail = jnp.where(lane == 0, high, jnp.where(lane == 1, counts - high, 0.0))
    out_ref[:, :D] = acc.astype(BF16)
    out_ref[:, D:] = tail.astype(BF16)


def sums_of(idx, parts, ps, ms, pieces):
    rows = X * COL
    return pl.pallas_call(
        functools.partial(sum_kernel, len(pieces), len(ps)),
        out_shape=(
            jax.ShapeDtypeStruct((K, WIDE), BF16),
            jax.ShapeDtypeStruct((X * 8, 128), F32),
        ),
        in_specs=[SMEM, VMEM] + [VMEM] * (2 * len(ps)) + [ANY] * len(pieces),
        out_specs=(VMEM, VMEM),
        scratch_shapes=[
            pltpu.VMEM((rows, D), BF16),
            pltpu.SemaphoreType.DMA((rows // CHUNK,)),
        ],
        compiler_params=pltpu.CompilerParams(vmem_limit_bytes=24 << 20),
        name="sums",
    )(idx, parts, *ps, *ms, *pieces)


def update_kernel(got_ref, cur_ref, new_ref, copies_ref, counts_ref):
    total = got_ref[pl.ds(0, OWN), :].astype(F32)
    for i in range(1, Z):
        total += got_ref[pl.ds(i * OWN, OWN), :].astype(F32)
    counts = total[:, D : D + 1] + total[:, D + 1 : D + 2]
    new = (total[:, :D] + cur_ref[...]) / (counts + 1.0)
    new_ref[...] = new
    for i in range(Z):
        copies_ref[pl.ds(i * OWN, OWN), :] = new.astype(BF16)
    row = lax.broadcasted_iota(jnp.int32, (OWN, OWN), 0)
    lane = lax.broadcasted_iota(jnp.int32, (OWN, OWN), 1)
    counts_ref[...] = jnp.sum(jnp.where(row == lane, counts, 0.0), axis=0, keepdims=True)


def update(got, current):
    return pl.pallas_call(
        update_kernel,
        out_shape=(
            jax.ShapeDtypeStruct((OWN, D), F32),
            jax.ShapeDtypeStruct((K, D), BF16),
            jax.ShapeDtypeStruct((1, OWN), F32),
        ),
        in_specs=[VMEM, VMEM],
        out_specs=(VMEM, VMEM, VMEM),
        name="update",
    )(got, current)


def shift(v, axis, size, k):
    return lax.ppermute(v, axis, [(i, (i + k) % size) for i in range(size)])


def on_device(embeddings, centroids):
    x, c = lax.axis_index("x"), lax.axis_index("c")
    idx = jnp.stack([x, c]).astype(jnp.int32)
    mine = lax.dynamic_slice_in_dim(embeddings, c * HALF, HALF, 0)
    near = {k: shift(mine, "x", X, k) for k in (1, 3, 2)}
    copies = jnp.tile(centroids.astype(BF16), (Z, 1))
    current = centroids
    for step in range(ITERS):
        cent = lax.all_to_all(copies, "z", 0, 0, tiled=True)
        if step == 0:
            p0, m0, l0 = score(idx, cent, [embeddings], 0)
            near, l0 = lax.optimization_barrier((near, l0))
            pieces = [embeddings]
            for k in (1, 2, 3):
                pieces += [near[k], shift(near[k], "c", C, 1)]
            p1, m1, lse = score(idx, cent, pieces[1:], 1, l0)
            ps, ms = [p0, p1], [m0, m1]
        else:
            p, m, lse = score(idx, cent, pieces, 0)
            ps, ms = [p], [m]
        lse = jnp.logaddexp2(lse, shift(lse, "c", C, 1))
        parts = lax.all_to_all(jnp.tile(lse, (X * Y, 1)), ("x", "y"), 0, 0, tiled=True)
        out, total = sums_of(idx, parts, ps, ms, pieces)
        got = lax.all_to_all(out, "z", 0, 0, tiled=True)
        current, copies, counts = update(got, current)
    row_lse = lax.dynamic_slice_in_dim(total, x * 8, 8, 0).reshape(COL) * math.log(2.0)
    return current, counts.reshape(OWN), row_lse


def solution(mesh):
    split = Mesh(mesh.devices.reshape(Z, X, Y, C), ("z", "x", "y", "c"))
    dp, every = ("z", "x"), ("z", "x", "y", "c")
    return jax.shard_map(
        on_device,
        mesh=split,
        in_specs=(P(dp, None), P(every, None)),
        out_specs=(P(every, None), P(every), P(dp)),
        check_vma=False,
    )
```

```python
import functools
import math

import jax
import jax.numpy as jnp
from jax import lax
from jax.experimental import pallas as pl
from jax.experimental.pallas import tpu as pltpu
from jax.sharding import Mesh
from jax.sharding import PartitionSpec as P

ITERS = 2
D = 768
Z, X, Y, C = 8, 4, 4, 2
OWN = 32
K = Z * OWN
COL = 1024
HALF, QUARTER = COL // 2, COL // 4
PACK = OWN * D // 128 + 16
F32, BF16 = jnp.float32, jnp.bfloat16
SCALE = 50.0 * math.log2(math.e)
VMEM = pl.BlockSpec(memory_space=pltpu.VMEM)
ANY = pl.BlockSpec(memory_space=pl.ANY)
PARTS = ((0,), (1, 3), (2,))
ROWS = tuple(COL * len(part) for part in PARTS)


def in_hbm(v):
    return pltpu.with_memory_space_constraint(v, pltpu.HBM)


def limit(mib):
    return pltpu.CompilerParams(vmem_limit_bytes=mib << 20)


def shape(*dims, dtype=F32):
    return jax.ShapeDtypeStruct(dims, dtype)


def rows_to_tile(v):
    return jnp.concatenate([v[:, i * 128 : (i + 1) * 128] for i in range(v.shape[1] // 128)], axis=0)


def tile_to_rows(v):
    return jnp.concatenate([v[i : i + 1] for i in range(v.shape[0])], axis=1)


def column_of(k, copy=0):
    return pl.ds(pl.multiple_of(32 * copy + 8 * lax.rem(lax.axis_index("x") + (X - k), X), 8), 8)


def prepare_kernel(emb_ref, cent_ref, mine_ref, copies_ref, cent, sems, cent_sem):
    read = pltpu.make_async_copy(cent_ref, cent, cent_sem)
    read.start()
    at = pl.multiple_of(lax.axis_index("c") * HALF, HALF)
    waits = []
    for i in range(0, HALF, 64):
        waits.append(
            pltpu.make_async_copy(
                emb_ref.at[pl.ds(at + i, 64)], mine_ref.at[pl.ds(i, 64)], sems.at[i // 64]
            )
        )
        waits[-1].start()
    read.wait()
    for i in range(Z):
        copies_ref[pl.ds(i * OWN, OWN), :] = cent[...].astype(BF16)
    for wait in waits:
        wait.wait()


def prepare(emb, cent):
    return pl.pallas_call(
        prepare_kernel,
        out_shape=(pltpu.VMEM((HALF, D), BF16), pltpu.VMEM((K, D), BF16)),
        in_specs=[ANY, ANY],
        out_specs=(VMEM,) * 2,
        scratch_shapes=[
            pltpu.VMEM((OWN, D), F32),
            pltpu.SemaphoreType.DMA((HALF // 64,)),
            pltpu.SemaphoreType.DMA,
        ],
        compiler_params=limit(4),
        name="prepare",
    )(in_hbm(emb), in_hbm(cent))


def relay_kernel(left_ref, right_ref, low_ref, high_ref):
    low_ref[...] = left_ref[pl.ds(0, QUARTER), :]
    high_ref[...] = right_ref[pl.ds(QUARTER, QUARTER), :]


def relay(left, right):
    return pl.pallas_call(
        relay_kernel,
        out_shape=(pltpu.VMEM((QUARTER, D), BF16),) * 2,
        in_specs=[VMEM] * 2,
        out_specs=(VMEM,) * 2,
        compiler_params=limit(4),
        name="relay",
    )(left, right)


def score_rows(cent, half_squares, emb, p_ref, m_ref):
    dots = lax.dot_general(cent, emb, (((1,), (1,)), ((), ())), preferred_element_type=F32)
    logits = dots * SCALE - half_squares
    peak = jnp.max(logits, axis=0, keepdims=True)
    p = jnp.exp2(logits - peak)
    total = jnp.sum(p, axis=0, keepdims=True)
    p_ref[...] = p.astype(BF16)
    m_ref[...] = rows_to_tile(peak)
    return rows_to_tile(peak + jnp.log2(total))


def half_squares_of(cent):
    wide = cent.astype(F32)
    return (0.5 * SCALE) * jnp.sum(wide * wide, axis=1, keepdims=True)


def spread(part, lse, lses_ref):
    for j, k in enumerate(part):
        for i in range(X * Y):
            lses_ref[column_of(k, i), :] = lse[8 * j : 8 * j + 8]


def arrive_kernel(part, before, cent_ref, *refs):
    emb, p_ref, m_ref, l_ref = refs[-4:]
    pieces = refs[: len(refs) - 4 - before]
    earlier = refs[len(pieces) : -4]
    c = lax.axis_index("c")
    cent = cent_ref[...].astype(BF16)
    half_squares = half_squares_of(cent)
    if part == (0,):
        emb[...] = pieces[0][...]
    else:
        size = pieces[0].shape[0]
        n = HALF // size
        for i, piece in enumerate(pieces):
            half = c if i // n % 2 == 0 else 1 - c
            at = pl.multiple_of(i // (2 * n) * COL + half * HALF + i % n * size, size)
            emb[pl.ds(at, size), :] = piece[...]
    lse = score_rows(cent, half_squares, emb[...], p_ref, m_ref)
    if before:
        spread(part, lse, l_ref)
        for other, ref in zip(PARTS, earlier):
            spread(other, ref[...], l_ref)
    else:
        l_ref[...] = lse


def arrive(cent, part, pieces, earlier=()):
    rows = COL * len(part)
    return pl.pallas_call(
        functools.partial(arrive_kernel, part, len(earlier)),
        out_shape=(
            pltpu.VMEM((rows, D), BF16),
            pltpu.VMEM((K, rows), BF16),
            pltpu.VMEM((rows // 128, 128), F32),
            shape(X * Y * 32 if earlier else rows // 128, 128),
        ),
        in_specs=[VMEM] * (1 + len(pieces) + len(earlier)),
        out_specs=(VMEM,) * 4,
        compiler_params=limit(16),
        name="arrive",
    )(cent, *pieces, *earlier)


def score_kernel(cent_ref, *refs):
    n = len(PARTS)
    embs, ps, ms, l_ref = refs[:n], refs[n : 2 * n], refs[2 * n : 3 * n], refs[3 * n]
    cent = cent_ref[...]
    half_squares = half_squares_of(cent)
    for part, emb, p_ref, m_ref in zip(PARTS, embs, ps, ms):
        spread(part, score_rows(cent, half_squares, emb[...], p_ref, m_ref), l_ref)


def score(cent, embs):
    n = len(PARTS)
    outs = pl.pallas_call(
        score_kernel,
        out_shape=(
            *(pltpu.VMEM((K, r), BF16) for r in ROWS),
            *(pltpu.VMEM((r // 128, 128), F32) for r in ROWS),
            shape(X * Y * 32, 128),
        ),
        in_specs=[VMEM] * (1 + n),
        out_specs=(VMEM,) * (2 * n + 1),
        compiler_params=limit(16),
        name="score",
    )(cent, *embs)
    return outs[:n], outs[n : 2 * n], outs[2 * n]


def sum_kernel(lses_ref, others_ref, *refs):
    n = len(PARTS)
    ps, ms, embs = refs[:n], refs[n : 2 * n], refs[2 * n : 3 * n]
    out_ref, row_ref, lse_ref = refs[3 * n :]
    lses = [r[pl.ds(i * 32, 32), :] for r in (lses_ref, others_ref) for i in range(X * Y)]
    peak = functools.reduce(jnp.maximum, lses)
    total = sum(jnp.exp2(v - peak) for v in lses)
    lse_ref[...] = peak + jnp.log2(total)
    row_ref[...] = lse_ref[column_of(0), :] * math.log(2.0)
    weights = jnp.zeros((K, 128), F32)
    sums = jnp.zeros((K, D), F32)
    for part, p_ref, m_ref, emb in zip(PARTS, ps, ms, embs):
        resps = []
        for j, k in enumerate(part):
            factor = tile_to_rows(jnp.exp2(m_ref[pl.ds(j * 8, 8), :] - lse_ref[column_of(k), :]))
            resp = (p_ref[:, pl.ds(j * COL, COL)].astype(F32) * factor).astype(BF16)
            wide = resp.astype(F32)
            for i in range(COL // 128):
                weights += wide[:, i * 128 : (i + 1) * 128]
            resps.append(resp)
        sums += jnp.dot(jnp.concatenate(resps, axis=1), emb[...], preferred_element_type=F32)
    counts = jnp.sum(weights, axis=1, keepdims=True)
    high = counts.astype(BF16).astype(F32)
    low = counts - high
    lane = lax.broadcasted_iota(jnp.int32, (16, 128), 1)
    for i in range(Z):
        for t in range(D // 128):
            out_ref[pl.ds(i * PACK + t * OWN, OWN), :] = sums[
                i * OWN : (i + 1) * OWN, t * 128 : (t + 1) * 128
            ].astype(BF16)
        tail = jnp.zeros((16, 128), F32)
        for q, v in enumerate((high, low)):
            for h in range(2):
                at = i * OWN + h * 16
                tail = jnp.where(lane == 2 * q + h, v[at : at + 16], tail)
        out_ref[pl.ds(i * PACK + PACK - 16, 16), :] = tail.astype(BF16)


def sums_of(lses, others, ps, ms, embs):
    n = len(PARTS)
    return pl.pallas_call(
        sum_kernel,
        out_shape=(shape(Z * PACK, 128, dtype=BF16), shape(8, 128)),
        in_specs=[VMEM] * (2 + 3 * n),
        out_specs=(VMEM, VMEM),
        scratch_shapes=[pltpu.VMEM((X * 8, 128), F32)],
        compiler_params=limit(16),
        name="sums",
    )(lses, others, *ps, *ms, *embs)


def update_kernel(last, got_ref, cur_ref, new_ref, out_ref):
    def total(at, n):
        return sum(got_ref[pl.ds(i * PACK + at, n), :].astype(F32) for i in range(Z))

    tail = total(PACK - 16, 16)
    tail = tail[:, :2] + tail[:, 2:4]
    counts = jnp.concatenate([tail[:, :1], tail[:, 1:]], axis=0)
    for t in range(D // 128):
        lanes = slice(t * 128, (t + 1) * 128)
        new = (total(t * OWN, OWN) + cur_ref[:, lanes]) / (counts + 1.0)
        new_ref[:, lanes] = new
        if not last:
            for i in range(Z):
                out_ref[pl.ds(i * OWN, OWN), lanes] = new.astype(BF16)
    if last:
        row = lax.broadcasted_iota(jnp.int32, (OWN, OWN), 0)
        lane = lax.broadcasted_iota(jnp.int32, (OWN, OWN), 1)
        out_ref[...] = jnp.sum(jnp.where(row == lane, counts, 0.0), axis=0, keepdims=True)


def update(got, current, last):
    return pl.pallas_call(
        functools.partial(update_kernel, last),
        out_shape=(shape(OWN, D), shape(1, OWN) if last else shape(K, D, dtype=BF16)),
        in_specs=[VMEM, VMEM],
        out_specs=(VMEM, VMEM),
        compiler_params=limit(8),
        name="update",
    )(got, current)


def shift(v, axis, size, k):
    return lax.ppermute(v, axis, [(i, (i + k) % size) for i in range(size)])


def swap(v):
    return shift(v, "c", C, 1)


def on_device(embeddings, centroids):
    mine, copies = prepare(embeddings, centroids)
    left, right = shift(mine, "x", X, 1), shift(mine, "x", X, 3)
    cent = lax.all_to_all(copies, "z", 0, 0, tiled=True)
    own = arrive(cent, PARTS[0], (embeddings,))
    left, right, first = lax.optimization_barrier((left, right, own[3]))
    low, high = relay(left, right)
    far_low, far_high = shift(low, "x", X, 1), shift(high, "x", X, 3)
    near = arrive(cent, PARTS[1], (left, swap(left), right, swap(right)))
    far_low, far_high, second = lax.optimization_barrier((far_low, far_high, near[3]))
    far = arrive(cent, PARTS[2], (far_low, far_high, swap(far_low), swap(far_high)), (first, second))
    embs, ps, ms, (_, _, lses) = zip(own, near, far)
    current = centroids
    for step in range(ITERS):
        if step > 0:
            cent = lax.all_to_all(out, "z", 0, 0, tiled=True)
            ps, ms, lses = score(cent, embs)
        lses = lax.all_to_all(lses, ("x", "y"), 0, 0, tiled=True)
        sums, row_lse = sums_of(lses, swap(lses), ps, ms, embs)
        got = lax.all_to_all(sums, "z", 0, 0, tiled=True)
        current, out = update(got, current, step == ITERS - 1)
    return current, out.reshape(OWN), row_lse.reshape(COL)


def solution(mesh):
    split = Mesh(mesh.devices.reshape(Z, X, Y, C), ("z", "x", "y", "c"))
    dp, every = ("z", "x"), ("z", "x", "y", "c")
    return jax.shard_map(
        on_device,
        mesh=split,
        in_specs=(P(dp, None), P(every, None)),
        out_specs=(P(every, None), P(every), P(dp)),
        check_vma=False,
    )
```

```python
import functools
import math

import jax
import jax.numpy as jnp
from jax import lax
from jax.experimental import pallas as pl
from jax.experimental.pallas import tpu as pltpu
from jax.sharding import Mesh
from jax.sharding import PartitionSpec as P

ITERS = 2
D = 768
Z, X, Y, C = 8, 4, 4, 2
OWN = 32
K = Z * OWN
COL = 1024
HALF, QUARTER = COL // 2, COL // 4
PACK = OWN * D // 128 + 16
F32, BF16 = jnp.float32, jnp.bfloat16
SCALE = 50.0 * math.log2(math.e)
VMEM = pl.BlockSpec(memory_space=pltpu.VMEM)
ANY = pl.BlockSpec(memory_space=pl.ANY)
PARTS = ((0,), (1, 3), (2,))
ROWS = tuple(COL * len(part) for part in PARTS)


def in_hbm(v):
    return pltpu.with_memory_space_constraint(v, pltpu.HBM)


def limit(mib):
    return pltpu.CompilerParams(vmem_limit_bytes=mib << 20)


def shape(*dims, dtype=F32):
    return jax.ShapeDtypeStruct(dims, dtype)


def rows_to_tile(v):
    return jnp.concatenate([v[:, i * 128 : (i + 1) * 128] for i in range(v.shape[1] // 128)], axis=0)


def tile_to_rows(v):
    return jnp.concatenate([v[i : i + 1] for i in range(v.shape[0])], axis=1)


def column_of(k):
    return pl.ds(pl.multiple_of(8 * lax.rem(lax.axis_index("x") + (X - k), X), 8), 8)


def prepare_kernel(emb_ref, cent_ref, mine_ref, copies_ref, cent, sems, cent_sem):
    read = pltpu.make_async_copy(cent_ref, cent, cent_sem)
    read.start()
    at = pl.multiple_of(lax.axis_index("c") * HALF, HALF)
    waits = []
    for i in range(0, HALF, 64):
        waits.append(
            pltpu.make_async_copy(
                emb_ref.at[pl.ds(at + i, 64)], mine_ref.at[pl.ds(i, 64)], sems.at[i // 64]
            )
        )
        waits[-1].start()
    read.wait()
    for i in range(Z):
        copies_ref[pl.ds(i * OWN, OWN), :] = cent[...].astype(BF16)
    for wait in waits:
        wait.wait()


def prepare(emb, cent):
    return pl.pallas_call(
        prepare_kernel,
        out_shape=(pltpu.VMEM((HALF, D), BF16), pltpu.VMEM((K, D), BF16)),
        in_specs=[ANY, ANY],
        out_specs=(VMEM,) * 2,
        scratch_shapes=[
            pltpu.VMEM((OWN, D), F32),
            pltpu.SemaphoreType.DMA((HALF // 64,)),
            pltpu.SemaphoreType.DMA,
        ],
        compiler_params=limit(4),
        name="prepare",
    )(in_hbm(emb), in_hbm(cent))


def relay_kernel(left_ref, right_ref, low_ref, high_ref):
    low_ref[...] = left_ref[pl.ds(0, QUARTER), :]
    high_ref[...] = right_ref[pl.ds(QUARTER, QUARTER), :]


def relay(left, right):
    return pl.pallas_call(
        relay_kernel,
        out_shape=(pltpu.VMEM((QUARTER, D), BF16),) * 2,
        in_specs=[VMEM] * 2,
        out_specs=(VMEM,) * 2,
        compiler_params=limit(4),
        name="relay",
    )(left, right)


def score_rows(cent, half_squares, emb, p_ref, m_ref):
    dots = lax.dot_general(cent, emb, (((1,), (1,)), ((), ())), preferred_element_type=F32)
    logits = dots * SCALE - half_squares
    peak = jnp.max(logits, axis=0, keepdims=True)
    p = jnp.exp2(logits - peak)
    total = jnp.sum(p, axis=0, keepdims=True)
    p_ref[...] = p.astype(BF16)
    m_ref[...] = rows_to_tile(peak)
    return rows_to_tile(peak + jnp.log2(total))


def half_squares_of(cent):
    wide = cent.astype(F32)
    return (0.5 * SCALE) * jnp.sum(wide * wide, axis=1, keepdims=True)


def spread(part, lse, lse_ref):
    for j, k in enumerate(part):
        lse_ref[column_of(k), :] = lse[8 * j : 8 * j + 8]


def arrive_kernel(part, before, cent_ref, *refs):
    emb, p_ref, m_ref, l_ref = refs[-4:]
    pieces = refs[: len(refs) - 4 - before]
    earlier = refs[len(pieces) : -4]
    c = lax.axis_index("c")
    cent = cent_ref[...].astype(BF16)
    half_squares = half_squares_of(cent)
    if part == (0,):
        emb[...] = pieces[0][...]
    else:
        size = pieces[0].shape[0]
        n = HALF // size
        for i, piece in enumerate(pieces):
            half = c if i // n % 2 == 0 else 1 - c
            at = pl.multiple_of(i // (2 * n) * COL + half * HALF + i % n * size, size)
            emb[pl.ds(at, size), :] = piece[...]
    lse = score_rows(cent, half_squares, emb[...], p_ref, m_ref)
    if before:
        spread(part, lse, l_ref)
        for other, ref in zip(PARTS, earlier):
            spread(other, ref[...], l_ref)
    else:
        l_ref[...] = lse


def arrive(cent, part, pieces, earlier=()):
    rows = COL * len(part)
    return pl.pallas_call(
        functools.partial(arrive_kernel, part, len(earlier)),
        out_shape=(
            pltpu.VMEM((rows, D), BF16),
            pltpu.VMEM((K, rows), BF16),
            pltpu.VMEM((rows // 128, 128), F32),
            pltpu.VMEM((X * 8 if earlier else rows // 128, 128), F32),
        ),
        in_specs=[VMEM] * (1 + len(pieces) + len(earlier)),
        out_specs=(VMEM,) * 4,
        compiler_params=limit(16),
        name="arrive",
    )(cent, *pieces, *earlier)


def score_kernel(cent_ref, *refs):
    n = len(PARTS)
    embs, ps, ms, l_ref = refs[:n], refs[n : 2 * n], refs[2 * n : 3 * n], refs[3 * n]
    cent = cent_ref[...]
    half_squares = half_squares_of(cent)
    for part, emb, p_ref, m_ref in zip(PARTS, embs, ps, ms):
        spread(part, score_rows(cent, half_squares, emb[...], p_ref, m_ref), l_ref)


def score(cent, embs):
    n = len(PARTS)
    outs = pl.pallas_call(
        score_kernel,
        out_shape=(
            *(pltpu.VMEM((K, r), BF16) for r in ROWS),
            *(pltpu.VMEM((r // 128, 128), F32) for r in ROWS),
            pltpu.VMEM((X * 8, 128), F32),
        ),
        in_specs=[VMEM] * (1 + n),
        out_specs=(VMEM,) * (2 * n + 1),
        compiler_params=limit(16),
        name="score",
    )(cent, *embs)
    return outs[:n], outs[n : 2 * n], outs[2 * n]


def combine_kernel(a_ref, b_ref, out_ref):
    a, b = a_ref[...], b_ref[...]
    peak = jnp.maximum(a, b)
    both = peak + jnp.log2(jnp.exp2(a - peak) + jnp.exp2(b - peak))
    for i in range(X * Y):
        out_ref[pl.ds(i * 32, 32), :] = both


def combine(a, b):
    return pl.pallas_call(
        combine_kernel,
        out_shape=pltpu.VMEM((X * Y * 32, 128), F32),
        in_specs=[VMEM] * 2,
        out_specs=VMEM,
        compiler_params=limit(2),
        name="combine",
    )(a, b)


def sum_kernel(lses_ref, *refs):
    n = len(PARTS)
    ps, ms, embs = refs[:n], refs[n : 2 * n], refs[2 * n : 3 * n]
    out_ref, row_ref, lse_ref = refs[3 * n :]
    lses = [lses_ref[pl.ds(i * 32, 32), :] for i in range(X * Y)]
    peak = functools.reduce(jnp.maximum, lses)
    total = sum(jnp.exp2(v - peak) for v in lses)
    lse_ref[...] = peak + jnp.log2(total)
    row_ref[...] = lse_ref[column_of(0), :] * math.log(2.0)
    weights = jnp.zeros((K, 128), F32)
    sums = jnp.zeros((K, D), F32)
    for part, p_ref, m_ref, emb in zip(PARTS, ps, ms, embs):
        resps = []
        for j, k in enumerate(part):
            factor = tile_to_rows(jnp.exp2(m_ref[pl.ds(j * 8, 8), :] - lse_ref[column_of(k), :]))
            resp = (p_ref[:, pl.ds(j * COL, COL)].astype(F32) * factor).astype(BF16)
            wide = resp.astype(F32)
            for i in range(COL // 128):
                weights += wide[:, i * 128 : (i + 1) * 128]
            resps.append(resp)
        sums += jnp.dot(jnp.concatenate(resps, axis=1), emb[...], preferred_element_type=F32)
    counts = jnp.sum(weights, axis=1, keepdims=True)
    high = counts.astype(BF16).astype(F32)
    low = counts - high
    lane = lax.broadcasted_iota(jnp.int32, (16, 128), 1)
    for i in range(Z):
        for t in range(D // 128):
            out_ref[pl.ds(i * PACK + t * OWN, OWN), :] = sums[
                i * OWN : (i + 1) * OWN, t * 128 : (t + 1) * 128
            ].astype(BF16)
        tail = jnp.zeros((16, 128), F32)
        for q, v in enumerate((high, low)):
            for h in range(2):
                at = i * OWN + h * 16
                tail = jnp.where(lane == 2 * q + h, v[at : at + 16], tail)
        out_ref[pl.ds(i * PACK + PACK - 16, 16), :] = tail.astype(BF16)


def sums_of(lses, ps, ms, embs):
    n = len(PARTS)
    return pl.pallas_call(
        sum_kernel,
        out_shape=(shape(Z * PACK, 128, dtype=BF16), shape(8, 128)),
        in_specs=[VMEM] * (1 + 3 * n),
        out_specs=(VMEM, VMEM),
        scratch_shapes=[pltpu.VMEM((X * 8, 128), F32)],
        compiler_params=limit(16),
        name="sums",
    )(lses, *ps, *ms, *embs)


def update_kernel(last, got_ref, cur_ref, new_ref, out_ref):
    def total(at, n):
        return sum(got_ref[pl.ds(i * PACK + at, n), :].astype(F32) for i in range(Z))

    tail = total(PACK - 16, 16)
    tail = tail[:, :2] + tail[:, 2:4]
    counts = jnp.concatenate([tail[:, :1], tail[:, 1:]], axis=0)
    for t in range(D // 128):
        lanes = slice(t * 128, (t + 1) * 128)
        new = (total(t * OWN, OWN) + cur_ref[:, lanes]) / (counts + 1.0)
        new_ref[:, lanes] = new
        if not last:
            for i in range(Z):
                out_ref[pl.ds(i * OWN, OWN), lanes] = new.astype(BF16)
    if last:
        row = lax.broadcasted_iota(jnp.int32, (OWN, OWN), 0)
        lane = lax.broadcasted_iota(jnp.int32, (OWN, OWN), 1)
        out_ref[...] = jnp.sum(jnp.where(row == lane, counts, 0.0), axis=0, keepdims=True)


def update(got, current, last):
    return pl.pallas_call(
        functools.partial(update_kernel, last),
        out_shape=(shape(OWN, D), shape(1, OWN) if last else shape(K, D, dtype=BF16)),
        in_specs=[VMEM, VMEM],
        out_specs=(VMEM, VMEM),
        compiler_params=limit(8),
        name="update",
    )(got, current)


def shift(v, axis, size, k):
    return lax.ppermute(v, axis, [(i, (i + k) % size) for i in range(size)])


def swap(v):
    return shift(v, "c", C, 1)


def exchange(v, axes, n):
    second = list(range(n))[::-1]
    groups = [[C * i for i in range(n)], [C * i + 1 for i in second]]
    return lax.all_to_all(v, (*axes, "c"), 0, 0, axis_index_groups=groups, tiled=True)


def on_device(embeddings, centroids):
    mine, copies = prepare(embeddings, centroids)
    left, right = shift(mine, "x", X, 1), shift(mine, "x", X, 3)
    cent = exchange(copies, ("z",), Z)
    own = arrive(cent, PARTS[0], (embeddings,))
    left, right, first = lax.optimization_barrier((left, right, own[3]))
    low, high = relay(left, right)
    far_low, far_high = shift(low, "x", X, 1), shift(high, "x", X, 3)
    near = arrive(cent, PARTS[1], (left, swap(left), right, swap(right)))
    far_low, far_high, second = lax.optimization_barrier((far_low, far_high, near[3]))
    far = arrive(cent, PARTS[2], (far_low, far_high, swap(far_low), swap(far_high)), (first, second))
    embs, ps, ms, (_, _, lse) = zip(own, near, far)
    current = centroids
    for step in range(ITERS):
        if step > 0:
            cent = exchange(out, ("z",), Z)
            ps, ms, lse = score(cent, embs)
        lses = exchange(combine(lse, swap(lse)), ("x", "y"), X * Y)
        sums, row_lse = sums_of(lses, ps, ms, embs)
        got = exchange(sums, ("z",), Z)
        current, out = update(got, current, step == ITERS - 1)
    return current, out.reshape(OWN), row_lse.reshape(COL)


def solution(mesh):
    split = Mesh(mesh.devices.reshape(Z, X, Y, C), ("z", "x", "y", "c"))
    dp, every = ("z", "x"), ("z", "x", "y", "c")
    return jax.shard_map(
        on_device,
        mesh=split,
        in_specs=(P(dp, None), P(every, None)),
        out_specs=(P(every, None), P(every), P(dp)),
        check_vma=False,
    )
```

```python
import functools
import math

import jax
import jax.numpy as jnp
from jax import lax
from jax.experimental import pallas as pl
from jax.experimental.pallas import tpu as pltpu
from jax.sharding import Mesh
from jax.sharding import PartitionSpec as P

ITERS = 2
D = 768
Z, X, Y, C = 8, 4, 4, 2
OWN = 32
K = Z * OWN
COL = 1024
HALF, QUARTER = COL // 2, COL // 4
PACK = OWN * D // 128 + 16
F32, BF16 = jnp.float32, jnp.bfloat16
SCALE = 50.0 * math.log2(math.e)
VMEM = pl.BlockSpec(memory_space=pltpu.VMEM)
ANY = pl.BlockSpec(memory_space=pl.ANY)
RING = ((0, 4, 2, 6, 1, 5, 3, 7), (7, 3, 5, 1, 6, 2, 4, 0))
PLANE = (tuple(range(X * Y)), tuple(range(X * Y))[::-1])
PARTS = ((0,), (1, 3), (2,))
ROWS = tuple(COL * len(part) for part in PARTS)


def in_hbm(v):
    return pltpu.with_memory_space_constraint(v, pltpu.HBM)


def limit(mib):
    return pltpu.CompilerParams(vmem_limit_bytes=mib << 20)


def shape(*dims, dtype=F32):
    return jax.ShapeDtypeStruct(dims, dtype)


def rows_to_tile(v):
    return jnp.concatenate([v[:, i * 128 : (i + 1) * 128] for i in range(v.shape[1] // 128)], axis=0)


def tile_to_rows(v):
    return jnp.concatenate([v[i : i + 1] for i in range(v.shape[0])], axis=1)


def column_of(k):
    return pl.ds(pl.multiple_of(8 * lax.rem(lax.axis_index("x") + (X - k), X), 8), 8)


def prepare_kernel(emb_ref, cent_ref, mine_ref, copies_ref, cent, sems, cent_sem):
    read = pltpu.make_async_copy(cent_ref, cent, cent_sem)
    read.start()
    at = pl.multiple_of(lax.axis_index("c") * HALF, HALF)
    waits = []
    for i in range(0, HALF, 64):
        waits.append(
            pltpu.make_async_copy(
                emb_ref.at[pl.ds(at + i, 64)], mine_ref.at[pl.ds(i, 64)], sems.at[i // 64]
            )
        )
        waits[-1].start()
    read.wait()
    for i in range(Z):
        copies_ref[pl.ds(i * OWN, OWN), :] = cent[...].astype(BF16)
    for wait in waits:
        wait.wait()


def prepare(emb, cent):
    return pl.pallas_call(
        prepare_kernel,
        out_shape=(pltpu.VMEM((HALF, D), BF16), pltpu.VMEM((K, D), BF16)),
        in_specs=[ANY, ANY],
        out_specs=(VMEM,) * 2,
        scratch_shapes=[
            pltpu.VMEM((OWN, D), F32),
            pltpu.SemaphoreType.DMA((HALF // 64,)),
            pltpu.SemaphoreType.DMA,
        ],
        compiler_params=limit(4),
        name="prepare",
    )(in_hbm(emb), in_hbm(cent))


def relay_kernel(left_ref, right_ref, low_ref, high_ref):
    low_ref[...] = left_ref[pl.ds(0, QUARTER), :]
    high_ref[...] = right_ref[pl.ds(QUARTER, QUARTER), :]


def relay(left, right):
    return pl.pallas_call(
        relay_kernel,
        out_shape=(pltpu.VMEM((QUARTER, D), BF16),) * 2,
        in_specs=[VMEM] * 2,
        out_specs=(VMEM,) * 2,
        compiler_params=limit(4),
        name="relay",
    )(left, right)


def score_rows(cent, half_squares, emb, p_ref, m_ref):
    dots = lax.dot_general(cent, emb, (((1,), (1,)), ((), ())), preferred_element_type=F32)
    logits = dots * SCALE - half_squares
    peak = jnp.max(logits, axis=0, keepdims=True)
    p = jnp.exp2(logits - peak)
    total = jnp.sum(p, axis=0, keepdims=True)
    p_ref[...] = p.astype(BF16)
    m_ref[...] = rows_to_tile(peak)
    return rows_to_tile(peak + jnp.log2(total))


def half_squares_of(cent):
    wide = cent.astype(F32)
    return (0.5 * SCALE) * jnp.sum(wide * wide, axis=1, keepdims=True)


def spread(part, lse, lse_ref):
    for j, k in enumerate(part):
        lse_ref[column_of(k), :] = lse[8 * j : 8 * j + 8]


def arrive_kernel(part, before, cent_ref, *refs):
    emb, p_ref, m_ref, l_ref = refs[-4:]
    pieces = refs[: len(refs) - 4 - before]
    earlier = refs[len(pieces) : -4]
    c = lax.axis_index("c")
    cent = cent_ref[...].astype(BF16)
    half_squares = half_squares_of(cent)
    if part == (0,):
        emb[...] = pieces[0][...]
    else:
        size = pieces[0].shape[0]
        n = HALF // size
        for i, piece in enumerate(pieces):
            half = c if i // n % 2 == 0 else 1 - c
            at = pl.multiple_of(i // (2 * n) * COL + half * HALF + i % n * size, size)
            emb[pl.ds(at, size), :] = piece[...]
    lse = score_rows(cent, half_squares, emb[...], p_ref, m_ref)
    if before:
        spread(part, lse, l_ref)
        for other, ref in zip(PARTS, earlier):
            spread(other, ref[...], l_ref)
    else:
        l_ref[...] = lse


def arrive(cent, part, pieces, earlier=()):
    rows = COL * len(part)
    return pl.pallas_call(
        functools.partial(arrive_kernel, part, len(earlier)),
        out_shape=(
            pltpu.VMEM((rows, D), BF16),
            pltpu.VMEM((K, rows), BF16),
            pltpu.VMEM((rows // 128, 128), F32),
            pltpu.VMEM((X * 8 if earlier else rows // 128, 128), F32),
        ),
        in_specs=[VMEM] * (1 + len(pieces) + len(earlier)),
        out_specs=(VMEM,) * 4,
        compiler_params=limit(16),
        name="arrive",
    )(cent, *pieces, *earlier)


def score_kernel(cent_ref, *refs):
    n = len(PARTS)
    embs, ps, ms, l_ref = refs[:n], refs[n : 2 * n], refs[2 * n : 3 * n], refs[3 * n]
    cent = cent_ref[...]
    half_squares = half_squares_of(cent)
    for part, emb, p_ref, m_ref in zip(PARTS, embs, ps, ms):
        spread(part, score_rows(cent, half_squares, emb[...], p_ref, m_ref), l_ref)


def score(cent, embs):
    n = len(PARTS)
    outs = pl.pallas_call(
        score_kernel,
        out_shape=(
            *(pltpu.VMEM((K, r), BF16) for r in ROWS),
            *(pltpu.VMEM((r // 128, 128), F32) for r in ROWS),
            pltpu.VMEM((X * 8, 128), F32),
        ),
        in_specs=[VMEM] * (1 + n),
        out_specs=(VMEM,) * (2 * n + 1),
        compiler_params=limit(16),
        name="score",
    )(cent, *embs)
    return outs[:n], outs[n : 2 * n], outs[2 * n]


def combine_kernel(a_ref, b_ref, out_ref):
    a, b = a_ref[...], b_ref[...]
    peak = jnp.maximum(a, b)
    both = peak + jnp.log2(jnp.exp2(a - peak) + jnp.exp2(b - peak))
    for i in range(X * Y):
        out_ref[pl.ds(i * 32, 32), :] = both


def combine(a, b):
    return pl.pallas_call(
        combine_kernel,
        out_shape=pltpu.VMEM((X * Y * 32, 128), F32),
        in_specs=[VMEM] * 2,
        out_specs=VMEM,
        compiler_params=limit(2),
        name="combine",
    )(a, b)


def sum_kernel(lses_ref, *refs):
    n = len(PARTS)
    ps, ms, embs = refs[:n], refs[n : 2 * n], refs[2 * n : 3 * n]
    out_ref, row_ref, lse_ref = refs[3 * n :]
    lses = [lses_ref[pl.ds(i * 32, 32), :] for i in range(X * Y)]
    peak = functools.reduce(jnp.maximum, lses)
    total = sum(jnp.exp2(v - peak) for v in lses)
    lse_ref[...] = peak + jnp.log2(total)
    row_ref[...] = lse_ref[column_of(0), :] * math.log(2.0)
    weights = jnp.zeros((K, 128), F32)
    sums = jnp.zeros((K, D), F32)
    for part, p_ref, m_ref, emb in zip(PARTS, ps, ms, embs):
        resps = []
        for j, k in enumerate(part):
            factor = tile_to_rows(jnp.exp2(m_ref[pl.ds(j * 8, 8), :] - lse_ref[column_of(k), :]))
            resp = (p_ref[:, pl.ds(j * COL, COL)].astype(F32) * factor).astype(BF16)
            wide = resp.astype(F32)
            for i in range(COL // 128):
                weights += wide[:, i * 128 : (i + 1) * 128]
            resps.append(resp)
        sums += jnp.dot(jnp.concatenate(resps, axis=1), emb[...], preferred_element_type=F32)
    counts = jnp.sum(weights, axis=1, keepdims=True)
    high = counts.astype(BF16).astype(F32)
    low = counts - high
    lane = lax.broadcasted_iota(jnp.int32, (16, 128), 1)
    for i in range(Z):
        for t in range(D // 128):
            out_ref[pl.ds(i * PACK + t * OWN, OWN), :] = sums[
                i * OWN : (i + 1) * OWN, t * 128 : (t + 1) * 128
            ].astype(BF16)
        tail = jnp.zeros((16, 128), F32)
        for q, v in enumerate((high, low)):
            for h in range(2):
                at = i * OWN + h * 16
                tail = jnp.where(lane == 2 * q + h, v[at : at + 16], tail)
        out_ref[pl.ds(i * PACK + PACK - 16, 16), :] = tail.astype(BF16)


def sums_of(lses, ps, ms, embs):
    n = len(PARTS)
    return pl.pallas_call(
        sum_kernel,
        out_shape=(shape(Z * PACK, 128, dtype=BF16), shape(8, 128)),
        in_specs=[VMEM] * (1 + 3 * n),
        out_specs=(VMEM, VMEM),
        scratch_shapes=[pltpu.VMEM((X * 8, 128), F32)],
        compiler_params=limit(16),
        name="sums",
    )(lses, *ps, *ms, *embs)


def update_kernel(last, got_ref, cur_ref, new_ref, out_ref):
    def total(at, n):
        return sum(got_ref[pl.ds(i * PACK + at, n), :].astype(F32) for i in range(Z))

    tail = total(PACK - 16, 16)
    tail = tail[:, :2] + tail[:, 2:4]
    counts = jnp.concatenate([tail[:, :1], tail[:, 1:]], axis=0)
    for t in range(D // 128):
        lanes = slice(t * 128, (t + 1) * 128)
        new = (total(t * OWN, OWN) + cur_ref[:, lanes]) / (counts + 1.0)
        new_ref[:, lanes] = new
        if not last:
            for i in range(Z):
                out_ref[pl.ds(i * OWN, OWN), lanes] = new.astype(BF16)
    if last:
        row = lax.broadcasted_iota(jnp.int32, (OWN, OWN), 0)
        lane = lax.broadcasted_iota(jnp.int32, (OWN, OWN), 1)
        out_ref[...] = jnp.sum(jnp.where(row == lane, counts, 0.0), axis=0, keepdims=True)


def update(got, current, last):
    return pl.pallas_call(
        functools.partial(update_kernel, last),
        out_shape=(shape(OWN, D), shape(1, OWN) if last else shape(K, D, dtype=BF16)),
        in_specs=[VMEM, VMEM],
        out_specs=(VMEM, VMEM),
        compiler_params=limit(8),
        name="update",
    )(got, current)


def shift(v, axis, size, k):
    return lax.ppermute(v, axis, [(i, (i + k) % size) for i in range(size)])


def swap(v):
    return shift(v, "c", C, 1)


def exchange(v, axes, orders):
    groups = [[C * i + c for i in orders[c]] for c in range(C)]
    return lax.all_to_all(v, (*axes, "c"), 0, 0, axis_index_groups=groups, tiled=True)


def on_device(embeddings, centroids):
    mine, copies = prepare(embeddings, centroids)
    left, right = shift(mine, "x", X, 1), shift(mine, "x", X, 3)
    cent = exchange(copies, ("z",), RING)
    own = arrive(cent, PARTS[0], (embeddings,))
    left, right, first = lax.optimization_barrier((left, right, own[3]))
    low, high = relay(left, right)
    far_low, far_high = shift(low, "x", X, 1), shift(high, "x", X, 3)
    near = arrive(cent, PARTS[1], (left, swap(left), right, swap(right)))
    far_low, far_high, second = lax.optimization_barrier((far_low, far_high, near[3]))
    far = arrive(cent, PARTS[2], (far_low, far_high, swap(far_low), swap(far_high)), (first, second))
    embs, ps, ms, (_, _, lse) = zip(own, near, far)
    current = centroids
    for step in range(ITERS):
        if step > 0:
            cent = exchange(out, ("z",), RING)
            ps, ms, lse = score(cent, embs)
        lses = exchange(combine(lse, swap(lse)), ("x", "y"), PLANE)
        sums, row_lse = sums_of(lses, ps, ms, embs)
        got = exchange(sums, ("z",), RING)
        current, out = update(got, current, step == ITERS - 1)
    return current, out.reshape(OWN), row_lse.reshape(COL)


def solution(mesh):
    split = Mesh(mesh.devices.reshape(Z, X, Y, C), ("z", "x", "y", "c"))
    dp, every = ("z", "x"), ("z", "x", "y", "c")
    return jax.shard_map(
        on_device,
        mesh=split,
        in_specs=(P(dp, None), P(every, None)),
        out_specs=(P(every, None), P(every), P(dp)),
        check_vma=False,
    )
```

```python
import functools
import math

import jax
import jax.numpy as jnp
from jax import lax
from jax.experimental import pallas as pl
from jax.experimental.pallas import tpu as pltpu
from jax.sharding import Mesh
from jax.sharding import PartitionSpec as P

ITERS = 2
D = 768
Z, X, Y, C = 8, 4, 4, 2
OWN = 32
K = Z * OWN
COL = 1024
HALF = COL // 2
QUARTER = HALF // Y
PACK = OWN * D // 128 + 16
F32, BF16 = jnp.float32, jnp.bfloat16
SCALE = 50.0 * math.log2(math.e)
VMEM = pl.BlockSpec(memory_space=pltpu.VMEM)
ANY = pl.BlockSpec(memory_space=pl.ANY)
RING = ((0, 4, 2, 6, 1, 5, 3, 7), (7, 3, 5, 1, 6, 2, 4, 0))
PLANE = (tuple(range(X * Y)), tuple(range(X * Y))[::-1])
PARTS = ((0,), (1, 3), (2,))
ROWS = tuple(COL * len(part) for part in PARTS)


def in_hbm(v):
    return pltpu.with_memory_space_constraint(v, pltpu.HBM)


def limit(mib):
    return pltpu.CompilerParams(vmem_limit_bytes=mib << 20)


def shape(*dims, dtype=F32):
    return jax.ShapeDtypeStruct(dims, dtype)


def rows_to_tile(v):
    return jnp.concatenate([v[:, i * 128 : (i + 1) * 128] for i in range(v.shape[1] // 128)], axis=0)


def tile_to_rows(v):
    return jnp.concatenate([v[i : i + 1] for i in range(v.shape[0])], axis=1)


def column_of(k):
    return pl.ds(pl.multiple_of(8 * lax.rem(lax.axis_index("x") + (X - k), X), 8), 8)


def quarter_kernel(emb_ref, quarter_ref, sems):
    at = lax.axis_index("c") * HALF + lax.axis_index("y") * QUARTER
    waits = []
    for i in range(0, QUARTER, 32):
        rows = pl.ds(pl.multiple_of(at + i, 32), 32)
        waits.append(pltpu.make_async_copy(emb_ref.at[rows], quarter_ref.at[pl.ds(i, 32)], sems.at[i // 32]))
        waits[-1].start()
    for wait in waits:
        wait.wait()


def quarter_of(emb):
    return pl.pallas_call(
        quarter_kernel,
        out_shape=pltpu.VMEM((QUARTER, D), BF16),
        in_specs=[ANY],
        out_specs=VMEM,
        scratch_shapes=[pltpu.SemaphoreType.DMA((QUARTER // 32,))],
        compiler_params=limit(4),
        name="quarter",
    )(in_hbm(emb))


def prepare_kernel(emb_ref, cent_ref, mine_ref, copies_ref, cent, sems, cent_sem):
    read = pltpu.make_async_copy(cent_ref, cent, cent_sem)
    read.start()
    at = pl.multiple_of(lax.axis_index("c") * HALF, HALF)
    waits = []
    for i in range(0, HALF, 64):
        waits.append(
            pltpu.make_async_copy(
                emb_ref.at[pl.ds(at + i, 64)], mine_ref.at[pl.ds(i, 64)], sems.at[i // 64]
            )
        )
        waits[-1].start()
    read.wait()
    for i in range(Z):
        copies_ref[pl.ds(i * OWN, OWN), :] = cent[...].astype(BF16)
    for wait in waits:
        wait.wait()


def prepare(emb, cent):
    return pl.pallas_call(
        prepare_kernel,
        out_shape=(pltpu.VMEM((HALF, D), BF16), pltpu.VMEM((K, D), BF16)),
        in_specs=[ANY, ANY],
        out_specs=(VMEM,) * 2,
        scratch_shapes=[
            pltpu.VMEM((OWN, D), F32),
            pltpu.SemaphoreType.DMA((HALF // 64,)),
            pltpu.SemaphoreType.DMA,
        ],
        compiler_params=limit(4),
        name="prepare",
    )(in_hbm(emb), in_hbm(cent))


def join_kernel(*refs):
    y = lax.axis_index("y")
    for i, ref in enumerate(refs[:-1]):
        at = pl.multiple_of(QUARTER * lax.rem(y + (Y - i), Y), QUARTER)
        refs[-1][pl.ds(at, QUARTER), :] = ref[...]


def join(quarters):
    return pl.pallas_call(
        join_kernel,
        out_shape=pltpu.VMEM((HALF, D), BF16),
        in_specs=[VMEM] * Y,
        out_specs=VMEM,
        compiler_params=limit(4),
        name="join",
    )(*quarters)


def score_rows(cent, half_squares, emb, p_ref, m_ref):
    dots = lax.dot_general(cent, emb, (((1,), (1,)), ((), ())), preferred_element_type=F32)
    logits = dots * SCALE - half_squares
    peak = jnp.max(logits, axis=0, keepdims=True)
    p = jnp.exp2(logits - peak)
    total = jnp.sum(p, axis=0, keepdims=True)
    p_ref[...] = p.astype(BF16)
    m_ref[...] = rows_to_tile(peak)
    return rows_to_tile(peak + jnp.log2(total))


def half_squares_of(cent):
    wide = cent.astype(F32)
    return (0.5 * SCALE) * jnp.sum(wide * wide, axis=1, keepdims=True)


def spread(part, lse, lse_ref):
    for j, k in enumerate(part):
        lse_ref[column_of(k), :] = lse[8 * j : 8 * j + 8]


def arrive_kernel(part, before, cent_ref, *refs):
    emb, p_ref, m_ref, l_ref = refs[-4:]
    pieces = refs[: len(refs) - 4 - before]
    earlier = refs[len(pieces) : -4]
    c = lax.axis_index("c")
    cent = cent_ref[...].astype(BF16)
    half_squares = half_squares_of(cent)
    if part == (0,):
        emb[...] = pieces[0][...]
    else:
        size = pieces[0].shape[0]
        n = HALF // size
        for i, piece in enumerate(pieces):
            half = c if i // n % 2 == 0 else 1 - c
            at = pl.multiple_of(i // (2 * n) * COL + half * HALF + i % n * size, size)
            emb[pl.ds(at, size), :] = piece[...]
    lse = score_rows(cent, half_squares, emb[...], p_ref, m_ref)
    if before:
        spread(part, lse, l_ref)
        for other, ref in zip(PARTS, earlier):
            spread(other, ref[...], l_ref)
    else:
        l_ref[...] = lse


def arrive(cent, part, pieces, earlier=()):
    rows = COL * len(part)
    return pl.pallas_call(
        functools.partial(arrive_kernel, part, len(earlier)),
        out_shape=(
            pltpu.VMEM((rows, D), BF16),
            pltpu.VMEM((K, rows), BF16),
            pltpu.VMEM((rows // 128, 128), F32),
            pltpu.VMEM((X * 8 if earlier else rows // 128, 128), F32),
        ),
        in_specs=[VMEM] * (1 + len(pieces) + len(earlier)),
        out_specs=(VMEM,) * 4,
        compiler_params=limit(16),
        name="arrive",
    )(cent, *pieces, *earlier)


def score_kernel(cent_ref, *refs):
    n = len(PARTS)
    embs, ps, ms, l_ref = refs[:n], refs[n : 2 * n], refs[2 * n : 3 * n], refs[3 * n]
    cent = cent_ref[...]
    half_squares = half_squares_of(cent)
    for part, emb, p_ref, m_ref in zip(PARTS, embs, ps, ms):
        spread(part, score_rows(cent, half_squares, emb[...], p_ref, m_ref), l_ref)


def score(cent, embs):
    n = len(PARTS)
    outs = pl.pallas_call(
        score_kernel,
        out_shape=(
            *(pltpu.VMEM((K, r), BF16) for r in ROWS),
            *(pltpu.VMEM((r // 128, 128), F32) for r in ROWS),
            pltpu.VMEM((X * 8, 128), F32),
        ),
        in_specs=[VMEM] * (1 + n),
        out_specs=(VMEM,) * (2 * n + 1),
        compiler_params=limit(16),
        name="score",
    )(cent, *embs)
    return outs[:n], outs[n : 2 * n], outs[2 * n]


def combine_kernel(a_ref, b_ref, out_ref):
    a, b = a_ref[...], b_ref[...]
    peak = jnp.maximum(a, b)
    both = peak + jnp.log2(jnp.exp2(a - peak) + jnp.exp2(b - peak))
    for i in range(X * Y):
        out_ref[pl.ds(i * 32, 32), :] = both


def combine(a, b):
    return pl.pallas_call(
        combine_kernel,
        out_shape=pltpu.VMEM((X * Y * 32, 128), F32),
        in_specs=[VMEM] * 2,
        out_specs=VMEM,
        compiler_params=limit(2),
        name="combine",
    )(a, b)


def sum_kernel(lses_ref, *refs):
    n = len(PARTS)
    ps, ms, embs = refs[:n], refs[n : 2 * n], refs[2 * n : 3 * n]
    out_ref, row_ref, lse_ref = refs[3 * n :]
    lses = [lses_ref[pl.ds(i * 32, 32), :] for i in range(X * Y)]
    peak = functools.reduce(jnp.maximum, lses)
    total = sum(jnp.exp2(v - peak) for v in lses)
    lse_ref[...] = peak + jnp.log2(total)
    row_ref[...] = lse_ref[column_of(0), :] * math.log(2.0)
    weights = jnp.zeros((K, 128), F32)
    sums = jnp.zeros((K, D), F32)
    for part, p_ref, m_ref, emb in zip(PARTS, ps, ms, embs):
        resps = []
        for j, k in enumerate(part):
            factor = tile_to_rows(jnp.exp2(m_ref[pl.ds(j * 8, 8), :] - lse_ref[column_of(k), :]))
            resp = (p_ref[:, pl.ds(j * COL, COL)].astype(F32) * factor).astype(BF16)
            wide = resp.astype(F32)
            for i in range(COL // 128):
                weights += wide[:, i * 128 : (i + 1) * 128]
            resps.append(resp)
        sums += jnp.dot(jnp.concatenate(resps, axis=1), emb[...], preferred_element_type=F32)
    counts = jnp.sum(weights, axis=1, keepdims=True)
    high = counts.astype(BF16).astype(F32)
    low = counts - high
    lane = lax.broadcasted_iota(jnp.int32, (16, 128), 1)
    for i in range(Z):
        for t in range(D // 128):
            out_ref[pl.ds(i * PACK + t * OWN, OWN), :] = sums[
                i * OWN : (i + 1) * OWN, t * 128 : (t + 1) * 128
            ].astype(BF16)
        tail = jnp.zeros((16, 128), F32)
        for q, v in enumerate((high, low)):
            for h in range(2):
                at = i * OWN + h * 16
                tail = jnp.where(lane == 2 * q + h, v[at : at + 16], tail)
        out_ref[pl.ds(i * PACK + PACK - 16, 16), :] = tail.astype(BF16)


def sums_of(lses, ps, ms, embs):
    n = len(PARTS)
    return pl.pallas_call(
        sum_kernel,
        out_shape=(shape(Z * PACK, 128, dtype=BF16), shape(8, 128)),
        in_specs=[VMEM] * (1 + 3 * n),
        out_specs=(VMEM, VMEM),
        scratch_shapes=[pltpu.VMEM((X * 8, 128), F32)],
        compiler_params=limit(16),
        name="sums",
    )(lses, *ps, *ms, *embs)


def update_kernel(last, got_ref, cur_ref, new_ref, out_ref):
    def total(at, n):
        return sum(got_ref[pl.ds(i * PACK + at, n), :].astype(F32) for i in range(Z))

    tail = total(PACK - 16, 16)
    tail = tail[:, :2] + tail[:, 2:4]
    counts = jnp.concatenate([tail[:, :1], tail[:, 1:]], axis=0)
    for t in range(D // 128):
        lanes = slice(t * 128, (t + 1) * 128)
        new = (total(t * OWN, OWN) + cur_ref[:, lanes]) / (counts + 1.0)
        new_ref[:, lanes] = new
        if not last:
            for i in range(Z):
                out_ref[pl.ds(i * OWN, OWN), lanes] = new.astype(BF16)
    if last:
        row = lax.broadcasted_iota(jnp.int32, (OWN, OWN), 0)
        lane = lax.broadcasted_iota(jnp.int32, (OWN, OWN), 1)
        out_ref[...] = jnp.sum(jnp.where(row == lane, counts, 0.0), axis=0, keepdims=True)


def update(got, current, last):
    return pl.pallas_call(
        functools.partial(update_kernel, last),
        out_shape=(shape(OWN, D), shape(1, OWN) if last else shape(K, D, dtype=BF16)),
        in_specs=[VMEM, VMEM],
        out_specs=(VMEM, VMEM),
        compiler_params=limit(8),
        name="update",
    )(got, current)


def shift(v, axis, size, k):
    return lax.ppermute(v, axis, [(i, (i + k) % size) for i in range(size)])


def swap(v):
    return shift(v, "c", C, 1)


def exchange(v, axes, orders):
    groups = [[C * i + c for i in orders[c]] for c in range(C)]
    return lax.all_to_all(v, (*axes, "c"), 0, 0, axis_index_groups=groups, tiled=True)


def on_device(embeddings, centroids):
    far = shift(quarter_of(embeddings), "x", X, 2)
    mine, copies = prepare(embeddings, centroids)
    left, right = shift(mine, "x", X, 1), shift(mine, "x", X, 3)
    quarters = [shift(far, "y", Y, k) for k in range(1, Y)]
    copies, far = lax.optimization_barrier((copies, far))
    cent = exchange(copies, ("z",), RING)
    own = arrive(cent, PARTS[0], (embeddings,))
    left, right, quarters, first = lax.optimization_barrier((left, right, quarters, own[3]))
    far = join((far, *quarters))
    near = arrive(cent, PARTS[1], (left, swap(left), right, swap(right)))
    far = arrive(cent, PARTS[2], (far, swap(far)), (first, near[3]))
    embs, ps, ms, (_, _, lse) = zip(own, near, far)
    current = centroids
    for step in range(ITERS):
        if step > 0:
            cent = exchange(out, ("z",), RING)
            ps, ms, lse = score(cent, embs)
        lses = exchange(combine(lse, swap(lse)), ("x", "y"), PLANE)
        sums, row_lse = sums_of(lses, ps, ms, embs)
        got = exchange(sums, ("z",), RING)
        current, out = update(got, current, step == ITERS - 1)
    return current, out.reshape(OWN), row_lse.reshape(COL)


def solution(mesh):
    split = Mesh(mesh.devices.reshape(Z, X, Y, C), ("z", "x", "y", "c"))
    dp, every = ("z", "x"), ("z", "x", "y", "c")
    return jax.shard_map(
        on_device,
        mesh=split,
        in_specs=(P(dp, None), P(every, None)),
        out_specs=(P(every, None), P(every), P(dp)),
        check_vma=False,
    )
```

```python
import functools
import math

import jax
import jax.numpy as jnp
from jax import lax
from jax.experimental import pallas as pl
from jax.experimental.pallas import tpu as pltpu
from jax.sharding import Mesh
from jax.sharding import PartitionSpec as P

ITERS = 2
D = 768
Z, X, Y, C = 8, 4, 4, 2
OWN = 32
K = Z * OWN
COL = 1024
HALF = COL // 2
QUARTER = HALF // Y
PACK = OWN * D // 128 + 16
F32, BF16 = jnp.float32, jnp.bfloat16
SCALE = 50.0 * math.log2(math.e)
VMEM = pl.BlockSpec(memory_space=pltpu.VMEM)
ANY = pl.BlockSpec(memory_space=pl.ANY)
RING = ((0, 4, 2, 6, 1, 5, 3, 7), (7, 3, 5, 1, 6, 2, 4, 0))
PLANE = (tuple(range(X * Y)), tuple(range(X * Y))[::-1])
PARTS = ((0,), (1, 3), (2,))
ROWS = tuple(COL * len(part) for part in PARTS)


def in_hbm(v):
    return pltpu.with_memory_space_constraint(v, pltpu.HBM)


def limit(mib):
    return pltpu.CompilerParams(vmem_limit_bytes=mib << 20)


def shape(*dims, dtype=F32):
    return jax.ShapeDtypeStruct(dims, dtype)


def rows_to_tile(v):
    return jnp.concatenate([v[:, i * 128 : (i + 1) * 128] for i in range(v.shape[1] // 128)], axis=0)


def tile_to_rows(v):
    return jnp.concatenate([v[i : i + 1] for i in range(v.shape[0])], axis=1)


def column_of(k):
    return pl.ds(pl.multiple_of(8 * lax.rem(lax.axis_index("x") + (X - k), X), 8), 8)


def quarter_kernel(emb_ref, quarter_ref, sems):
    at = lax.axis_index("c") * HALF + lax.axis_index("y") * QUARTER
    waits = []
    for i in range(0, QUARTER, 32):
        rows = pl.ds(pl.multiple_of(at + i, 32), 32)
        waits.append(pltpu.make_async_copy(emb_ref.at[rows], quarter_ref.at[pl.ds(i, 32)], sems.at[i // 32]))
        waits[-1].start()
    for wait in waits:
        wait.wait()


def quarter_of(emb):
    return pl.pallas_call(
        quarter_kernel,
        out_shape=pltpu.VMEM((QUARTER, D), BF16),
        in_specs=[ANY],
        out_specs=VMEM,
        scratch_shapes=[pltpu.SemaphoreType.DMA((QUARTER // 32,))],
        compiler_params=limit(4),
        name="quarter",
    )(in_hbm(emb))


def prepare_kernel(emb_ref, cent_ref, mine_ref, copies_ref, cent, sems, cent_sem):
    read = pltpu.make_async_copy(cent_ref, cent, cent_sem)
    read.start()
    at = pl.multiple_of(lax.axis_index("c") * HALF, HALF)
    waits = []
    for i in range(0, HALF, 64):
        waits.append(
            pltpu.make_async_copy(
                emb_ref.at[pl.ds(at + i, 64)], mine_ref.at[pl.ds(i, 64)], sems.at[i // 64]
            )
        )
        waits[-1].start()
    read.wait()
    for i in range(Z):
        copies_ref[pl.ds(i * OWN, OWN), :] = cent[...].astype(BF16)
    for wait in waits:
        wait.wait()


def prepare(emb, cent):
    return pl.pallas_call(
        prepare_kernel,
        out_shape=(pltpu.VMEM((HALF, D), BF16), pltpu.VMEM((K, D), BF16)),
        in_specs=[ANY, ANY],
        out_specs=(VMEM,) * 2,
        scratch_shapes=[
            pltpu.VMEM((OWN, D), F32),
            pltpu.SemaphoreType.DMA((HALF // 64,)),
            pltpu.SemaphoreType.DMA,
        ],
        compiler_params=limit(4),
        name="prepare",
    )(in_hbm(emb), in_hbm(cent))


def join_kernel(*refs):
    y = lax.axis_index("y")
    for i, ref in enumerate(refs[:-1]):
        at = pl.multiple_of(QUARTER * lax.rem(y + (Y - i), Y), QUARTER)
        refs[-1][pl.ds(at, QUARTER), :] = ref[...]


def join(quarters):
    return pl.pallas_call(
        join_kernel,
        out_shape=pltpu.VMEM((HALF, D), BF16),
        in_specs=[VMEM] * Y,
        out_specs=VMEM,
        compiler_params=limit(4),
        name="join",
    )(*quarters)


def score_rows(cent, half_squares, emb, p_ref, m_ref):
    dots = lax.dot_general(cent, emb, (((1,), (1,)), ((), ())), preferred_element_type=F32)
    logits = dots * SCALE - half_squares
    peak = jnp.max(logits, axis=0, keepdims=True)
    p = jnp.exp2(logits - peak)
    total = jnp.sum(p, axis=0, keepdims=True)
    p_ref[...] = p.astype(BF16)
    m_ref[...] = rows_to_tile(peak)
    return rows_to_tile(peak + jnp.log2(total))


def half_squares_of(cent):
    wide = cent.astype(F32)
    return (0.5 * SCALE) * jnp.sum(wide * wide, axis=1, keepdims=True)


def spread(part, lse, lse_ref):
    for j, k in enumerate(part):
        lse_ref[column_of(k), :] = lse[8 * j : 8 * j + 8]


def arrive_kernel(part, before, cent_ref, *refs):
    emb, p_ref, m_ref, l_ref = refs[-4:]
    pieces = refs[: len(refs) - 4 - before]
    earlier = refs[len(pieces) : -4]
    c = lax.axis_index("c")
    cent = cent_ref[...].astype(BF16)
    half_squares = half_squares_of(cent)
    if part == (0,):
        emb[...] = pieces[0][...]
    else:
        size = pieces[0].shape[0]
        n = HALF // size
        for i, piece in enumerate(pieces):
            half = c if i // n % 2 == 0 else 1 - c
            at = pl.multiple_of(i // (2 * n) * COL + half * HALF + i % n * size, size)
            emb[pl.ds(at, size), :] = piece[...]
    lse = score_rows(cent, half_squares, emb[...], p_ref, m_ref)
    if before:
        spread(part, lse, l_ref)
        for other, ref in zip(PARTS, earlier):
            spread(other, ref[...], l_ref)
    else:
        l_ref[...] = lse


def arrive(cent, part, pieces, earlier=()):
    rows = COL * len(part)
    return pl.pallas_call(
        functools.partial(arrive_kernel, part, len(earlier)),
        out_shape=(
            pltpu.VMEM((rows, D), BF16),
            pltpu.VMEM((K, rows), BF16),
            pltpu.VMEM((rows // 128, 128), F32),
            pltpu.VMEM((X * 8 if earlier else rows // 128, 128), F32),
        ),
        in_specs=[VMEM] * (1 + len(pieces) + len(earlier)),
        out_specs=(VMEM,) * 4,
        compiler_params=limit(16),
        name="arrive",
    )(cent, *pieces, *earlier)


def score_kernel(cent_ref, *refs):
    n = len(PARTS)
    embs, ps, ms, l_ref = refs[:n], refs[n : 2 * n], refs[2 * n : 3 * n], refs[3 * n]
    cent = cent_ref[...]
    half_squares = half_squares_of(cent)
    for part, emb, p_ref, m_ref in zip(PARTS, embs, ps, ms):
        spread(part, score_rows(cent, half_squares, emb[...], p_ref, m_ref), l_ref)


def score(cent, embs):
    n = len(PARTS)
    outs = pl.pallas_call(
        score_kernel,
        out_shape=(
            *(pltpu.VMEM((K, r), BF16) for r in ROWS),
            *(pltpu.VMEM((r // 128, 128), F32) for r in ROWS),
            pltpu.VMEM((X * 8, 128), F32),
        ),
        in_specs=[VMEM] * (1 + n),
        out_specs=(VMEM,) * (2 * n + 1),
        compiler_params=limit(16),
        name="score",
    )(cent, *embs)
    return outs[:n], outs[n : 2 * n], outs[2 * n]


def combine_kernel(a_ref, b_ref, out_ref):
    a, b = a_ref[...], b_ref[...]
    peak = jnp.maximum(a, b)
    both = peak + jnp.log2(jnp.exp2(a - peak) + jnp.exp2(b - peak))
    for i in range(X * Y):
        out_ref[pl.ds(i * 32, 32), :] = both


def combine(a, b):
    return pl.pallas_call(
        combine_kernel,
        out_shape=pltpu.VMEM((X * Y * 32, 128), F32),
        in_specs=[VMEM] * 2,
        out_specs=VMEM,
        compiler_params=limit(2),
        name="combine",
    )(a, b)


def sum_kernel(last, lses_ref, *refs):
    n = len(PARTS)
    ps, ms, embs = refs[:n], refs[n : 2 * n], refs[2 * n : 3 * n]
    out_ref, lse_ref = refs[3 * n], refs[-1]
    lses = [lses_ref[pl.ds(i * 32, 32), :] for i in range(X * Y)]
    peak = functools.reduce(jnp.maximum, lses)
    total = sum(jnp.exp2(v - peak) for v in lses)
    lse_ref[...] = peak + jnp.log2(total)
    if last:
        refs[3 * n + 1][...] = lse_ref[column_of(0), :] * math.log(2.0)
    weights = jnp.zeros((K, 128), F32)
    sums = jnp.zeros((K, D), F32)
    for part, p_ref, m_ref, emb in zip(PARTS, ps, ms, embs):
        resps = []
        for j, k in enumerate(part):
            factor = tile_to_rows(jnp.exp2(m_ref[pl.ds(j * 8, 8), :] - lse_ref[column_of(k), :]))
            resp = (p_ref[:, pl.ds(j * COL, COL)].astype(F32) * factor).astype(BF16)
            wide = resp.astype(F32)
            for i in range(COL // 128):
                weights += wide[:, i * 128 : (i + 1) * 128]
            resps.append(resp)
        sums += jnp.dot(jnp.concatenate(resps, axis=1), emb[...], preferred_element_type=F32)
    counts = jnp.sum(weights, axis=1, keepdims=True)
    high = counts.astype(BF16).astype(F32)
    low = counts - high
    lane = lax.broadcasted_iota(jnp.int32, (16, 128), 1)
    for i in range(Z):
        for t in range(D // 128):
            out_ref[pl.ds(i * PACK + t * OWN, OWN), :] = sums[
                i * OWN : (i + 1) * OWN, t * 128 : (t + 1) * 128
            ].astype(BF16)
        tail = jnp.zeros((16, 128), F32)
        for q, v in enumerate((high, low)):
            for h in range(2):
                at = i * OWN + h * 16
                tail = jnp.where(lane == 2 * q + h, v[at : at + 16], tail)
        out_ref[pl.ds(i * PACK + PACK - 16, 16), :] = tail.astype(BF16)


def sums_of(lses, ps, ms, embs, last):
    n = len(PARTS)
    return pl.pallas_call(
        functools.partial(sum_kernel, last),
        out_shape=(pltpu.VMEM((Z * PACK, 128), BF16), *([pltpu.VMEM((8, 128), F32)] if last else [])),
        in_specs=[VMEM] * (1 + 3 * n),
        out_specs=(VMEM,) * (1 + last),
        scratch_shapes=[pltpu.VMEM((X * 8, 128), F32)],
        compiler_params=limit(16),
        name="sums",
    )(lses, *ps, *ms, *embs)


def update_kernel(last, got_ref, cur_ref, *refs):
    if last:
        lse_ref, new_ref, out_ref, row_ref = refs
        row_ref[...] = lse_ref[...]
    else:
        new_ref, out_ref = refs

    def total(at, n):
        return sum(got_ref[pl.ds(i * PACK + at, n), :].astype(F32) for i in range(Z))

    tail = total(PACK - 16, 16)
    tail = tail[:, :2] + tail[:, 2:4]
    counts = jnp.concatenate([tail[:, :1], tail[:, 1:]], axis=0)
    for t in range(D // 128):
        lanes = slice(t * 128, (t + 1) * 128)
        new = (total(t * OWN, OWN) + cur_ref[:, lanes]) / (counts + 1.0)
        new_ref[:, lanes] = new
        if not last:
            for i in range(Z):
                out_ref[pl.ds(i * OWN, OWN), lanes] = new.astype(BF16)
    if last:
        row = lax.broadcasted_iota(jnp.int32, (OWN, OWN), 0)
        lane = lax.broadcasted_iota(jnp.int32, (OWN, OWN), 1)
        out_ref[...] = jnp.sum(jnp.where(row == lane, counts, 0.0), axis=0, keepdims=True)


def update(got, current, row_lse=None):
    last = row_lse is not None
    return pl.pallas_call(
        functools.partial(update_kernel, last),
        out_shape=(
            (shape(OWN, D), shape(1, OWN), shape(8, 128)) if last else (shape(OWN, D), shape(K, D, dtype=BF16))
        ),
        in_specs=[VMEM] * (2 + last),
        out_specs=(VMEM,) * (2 + last),
        compiler_params=limit(8),
        name="update",
    )(got, current, *([row_lse] if last else []))


def shift(v, axis, size, k):
    return lax.ppermute(v, axis, [(i, (i + k) % size) for i in range(size)])


def swap(v):
    return shift(v, "c", C, 1)


def exchange(v, axes, orders):
    groups = [[C * i + c for i in orders[c]] for c in range(C)]
    return lax.all_to_all(v, (*axes, "c"), 0, 0, axis_index_groups=groups, tiled=True)


def on_device(embeddings, centroids):
    far = shift(quarter_of(embeddings), "x", X, 2)
    mine, copies = prepare(embeddings, centroids)
    left, right = shift(mine, "x", X, 1), shift(mine, "x", X, 3)
    quarters = [shift(far, "y", Y, k) for k in range(1, Y)]
    copies, far = lax.optimization_barrier((copies, far))
    cent = exchange(copies, ("z",), RING)
    own = arrive(cent, PARTS[0], (embeddings,))
    left, right, quarters, first = lax.optimization_barrier((left, right, quarters, own[3]))
    far = join((far, *quarters))
    near = arrive(cent, PARTS[1], (left, swap(left), right, swap(right)))
    far = arrive(cent, PARTS[2], (far, swap(far)), (first, near[3]))
    embs, ps, ms, (_, _, lse) = zip(own, near, far)
    current = centroids
    for step in range(ITERS):
        if step > 0:
            cent = exchange(out, ("z",), RING)
            ps, ms, lse = score(cent, embs)
        lses = exchange(combine(lse, swap(lse)), ("x", "y"), PLANE)
        last = step == ITERS - 1
        sums, *row_lse = sums_of(lses, ps, ms, embs, last)
        got = exchange(sums, ("z",), RING)
        if not last:
            current, out = update(got, current)
    current, counts, row_lse = update(got, current, row_lse[0])
    return current, counts.reshape(OWN), row_lse.reshape(COL)


def solution(mesh):
    split = Mesh(mesh.devices.reshape(Z, X, Y, C), ("z", "x", "y", "c"))
    dp, every = ("z", "x"), ("z", "x", "y", "c")
    return jax.shard_map(
        on_device,
        mesh=split,
        in_specs=(P(dp, None), P(every, None)),
        out_specs=(P(every, None), P(every), P(dp)),
        check_vma=False,
    )
```

```python
import functools
import math

import jax
import jax.numpy as jnp
from jax import lax
from jax.experimental import pallas as pl
from jax.experimental.pallas import tpu as pltpu
from jax.sharding import Mesh
from jax.sharding import PartitionSpec as P

ITERS = 2
D = 768
Z, X, Y, C = 8, 4, 4, 2
OWN = 32
K = Z * OWN
COL = 1024
HALF = COL // 2
QUARTER = HALF // Y
PACK = OWN * D // 128 + 16
F32, BF16 = jnp.float32, jnp.bfloat16
SCALE = 50.0 * math.log2(math.e)
VMEM = pl.BlockSpec(memory_space=pltpu.VMEM)
ANY = pl.BlockSpec(memory_space=pl.ANY)
RING = ((0, 4, 2, 6, 1, 5, 3, 7), (7, 3, 5, 1, 6, 2, 4, 0))
PLANE = (tuple(range(X * Y)), tuple(range(X * Y))[::-1])
PARTS = ((0,), (1, 3), (2,))
ROWS = tuple(COL * len(part) for part in PARTS)


def in_hbm(v):
    return pltpu.with_memory_space_constraint(v, pltpu.HBM)


def limit(mib):
    return pltpu.CompilerParams(vmem_limit_bytes=mib << 20)


def shape(*dims, dtype=F32):
    return jax.ShapeDtypeStruct(dims, dtype)


def rows_to_tile(v):
    return jnp.concatenate([v[:, i * 128 : (i + 1) * 128] for i in range(v.shape[1] // 128)], axis=0)


def tile_to_rows(v):
    return jnp.concatenate([v[i : i + 1] for i in range(v.shape[0])], axis=1)


def column_of(k):
    return pl.ds(pl.multiple_of(8 * lax.rem(lax.axis_index("x") + (X - k), X), 8), 8)


def quarter_kernel(emb_ref, quarter_ref, sems):
    at = lax.axis_index("c") * HALF + lax.axis_index("y") * QUARTER
    waits = []
    for i in range(0, QUARTER, 32):
        rows = pl.ds(pl.multiple_of(at + i, 32), 32)
        waits.append(pltpu.make_async_copy(emb_ref.at[rows], quarter_ref.at[pl.ds(i, 32)], sems.at[i // 32]))
        waits[-1].start()
    for wait in waits:
        wait.wait()


def quarter_of(emb):
    return pl.pallas_call(
        quarter_kernel,
        out_shape=pltpu.VMEM((QUARTER, D), BF16),
        in_specs=[ANY],
        out_specs=VMEM,
        scratch_shapes=[pltpu.SemaphoreType.DMA((QUARTER // 32,))],
        compiler_params=limit(4),
        name="quarter",
    )(in_hbm(emb))


def prepare_kernel(emb_ref, cent_ref, mine_ref, copies_ref, mine, cent, copies, sems, out_sems, cent_sem, copies_sem):
    read = pltpu.make_async_copy(cent_ref, cent, cent_sem)
    read.start()
    at = pl.multiple_of(lax.axis_index("c") * HALF, HALF)
    reads, writes = [], []
    for i in range(HALF // 64):
        rows = pl.ds(i * 64, 64)
        reads.append(pltpu.make_async_copy(emb_ref.at[pl.ds(at + i * 64, 64)], mine.at[rows], sems.at[i]))
        writes.append(pltpu.make_async_copy(mine.at[rows], mine_ref.at[rows], out_sems.at[i]))
        reads[-1].start()
    read.wait()
    for i in range(Z):
        copies[pl.ds(i * OWN, OWN), :] = cent[...].astype(BF16)
    writes.append(pltpu.make_async_copy(copies, copies_ref, copies_sem))
    writes[-1].start()
    for i in range(HALF // 64):
        reads[i].wait()
        writes[i].start()
    for write in writes:
        write.wait()


def prepare(emb, cent):
    return pl.pallas_call(
        prepare_kernel,
        out_shape=(pltpu.HBM((HALF, D), BF16), pltpu.HBM((K, D), BF16)),
        in_specs=[ANY, ANY],
        out_specs=(ANY,) * 2,
        scratch_shapes=[
            pltpu.VMEM((HALF, D), BF16),
            pltpu.VMEM((OWN, D), F32),
            pltpu.VMEM((K, D), BF16),
            pltpu.SemaphoreType.DMA((HALF // 64,)),
            pltpu.SemaphoreType.DMA((HALF // 64,)),
            pltpu.SemaphoreType.DMA,
            pltpu.SemaphoreType.DMA,
        ],
        compiler_params=limit(4),
        name="prepare",
    )(in_hbm(emb), in_hbm(cent))


def join_kernel(*refs):
    y = lax.axis_index("y")
    for i, ref in enumerate(refs[:-1]):
        at = pl.multiple_of(QUARTER * lax.rem(y + (Y - i), Y), QUARTER)
        refs[-1][pl.ds(at, QUARTER), :] = ref[...]


def join(quarters):
    return pl.pallas_call(
        join_kernel,
        out_shape=pltpu.VMEM((HALF, D), BF16),
        in_specs=[VMEM] * Y,
        out_specs=VMEM,
        compiler_params=limit(4),
        name="join",
    )(*quarters)


def score_rows(cent, half_squares, emb, p_ref, m_ref):
    dots = lax.dot_general(cent, emb, (((1,), (1,)), ((), ())), preferred_element_type=F32)
    logits = dots * SCALE - half_squares
    peak = jnp.max(logits, axis=0, keepdims=True)
    p = jnp.exp2(logits - peak)
    total = jnp.sum(p, axis=0, keepdims=True)
    p_ref[...] = p.astype(BF16)
    m_ref[...] = rows_to_tile(peak)
    return rows_to_tile(peak + jnp.log2(total))


def half_squares_of(cent):
    wide = cent.astype(F32)
    return (0.5 * SCALE) * jnp.sum(wide * wide, axis=1, keepdims=True)


def spread(part, lse, lse_ref):
    for j, k in enumerate(part):
        lse_ref[column_of(k), :] = lse[8 * j : 8 * j + 8]


def arrive_kernel(part, before, cent_ref, *refs):
    emb, p_ref, m_ref, l_ref = refs[-4:]
    pieces = refs[: len(refs) - 4 - before]
    earlier = refs[len(pieces) : -4]
    c = lax.axis_index("c")
    cent = cent_ref[...].astype(BF16)
    half_squares = half_squares_of(cent)
    if part == (0,):
        emb[...] = pieces[0][...]
    else:
        size = pieces[0].shape[0]
        n = HALF // size
        for i, piece in enumerate(pieces):
            half = c if i // n % 2 == 0 else 1 - c
            at = pl.multiple_of(i // (2 * n) * COL + half * HALF + i % n * size, size)
            emb[pl.ds(at, size), :] = piece[...]
    lse = score_rows(cent, half_squares, emb[...], p_ref, m_ref)
    if before:
        spread(part, lse, l_ref)
        for other, ref in zip(PARTS, earlier):
            spread(other, ref[...], l_ref)
    else:
        l_ref[...] = lse


def arrive(cent, part, pieces, earlier=()):
    rows = COL * len(part)
    return pl.pallas_call(
        functools.partial(arrive_kernel, part, len(earlier)),
        out_shape=(
            pltpu.VMEM((rows, D), BF16),
            pltpu.VMEM((K, rows), BF16),
            pltpu.VMEM((rows // 128, 128), F32),
            pltpu.VMEM((X * 8 if earlier else rows // 128, 128), F32),
        ),
        in_specs=[VMEM] * (1 + len(pieces) + len(earlier)),
        out_specs=(VMEM,) * 4,
        compiler_params=limit(16),
        name="arrive",
    )(cent, *pieces, *earlier)


def score_kernel(cent_ref, *refs):
    n = len(PARTS)
    embs, ps, ms, l_ref = refs[:n], refs[n : 2 * n], refs[2 * n : 3 * n], refs[3 * n]
    cent = cent_ref[...]
    half_squares = half_squares_of(cent)
    for part, emb, p_ref, m_ref in zip(PARTS, embs, ps, ms):
        spread(part, score_rows(cent, half_squares, emb[...], p_ref, m_ref), l_ref)


def score(cent, embs):
    n = len(PARTS)
    outs = pl.pallas_call(
        score_kernel,
        out_shape=(
            *(pltpu.VMEM((K, r), BF16) for r in ROWS),
            *(pltpu.VMEM((r // 128, 128), F32) for r in ROWS),
            pltpu.VMEM((X * 8, 128), F32),
        ),
        in_specs=[VMEM] * (1 + n),
        out_specs=(VMEM,) * (2 * n + 1),
        compiler_params=limit(16),
        name="score",
    )(cent, *embs)
    return outs[:n], outs[n : 2 * n], outs[2 * n]


def combine_kernel(a_ref, b_ref, out_ref):
    a, b = a_ref[...], b_ref[...]
    peak = jnp.maximum(a, b)
    both = peak + jnp.log2(jnp.exp2(a - peak) + jnp.exp2(b - peak))
    for i in range(X * Y):
        out_ref[pl.ds(i * 32, 32), :] = both


def combine(a, b):
    return pl.pallas_call(
        combine_kernel,
        out_shape=pltpu.VMEM((X * Y * 32, 128), F32),
        in_specs=[VMEM] * 2,
        out_specs=VMEM,
        compiler_params=limit(2),
        name="combine",
    )(a, b)


def sum_kernel(last, lses_ref, *refs):
    n = len(PARTS)
    ps, ms, embs = refs[:n], refs[n : 2 * n], refs[2 * n : 3 * n]
    out_ref, lse_ref = refs[3 * n], refs[-1]
    lses = [lses_ref[pl.ds(i * 32, 32), :] for i in range(X * Y)]
    peak = functools.reduce(jnp.maximum, lses)
    total = sum(jnp.exp2(v - peak) for v in lses)
    lse_ref[...] = peak + jnp.log2(total)
    if last:
        refs[3 * n + 1][...] = lse_ref[column_of(0), :] * math.log(2.0)
    weights = jnp.zeros((K, 128), F32)
    sums = jnp.zeros((K, D), F32)
    for part, p_ref, m_ref, emb in zip(PARTS, ps, ms, embs):
        resps = []
        for j, k in enumerate(part):
            factor = tile_to_rows(jnp.exp2(m_ref[pl.ds(j * 8, 8), :] - lse_ref[column_of(k), :]))
            resp = (p_ref[:, pl.ds(j * COL, COL)].astype(F32) * factor).astype(BF16)
            wide = resp.astype(F32)
            for i in range(COL // 128):
                weights += wide[:, i * 128 : (i + 1) * 128]
            resps.append(resp)
        sums += jnp.dot(jnp.concatenate(resps, axis=1), emb[...], preferred_element_type=F32)
    counts = jnp.sum(weights, axis=1, keepdims=True)
    high = counts.astype(BF16).astype(F32)
    low = counts - high
    lane = lax.broadcasted_iota(jnp.int32, (16, 128), 1)
    for i in range(Z):
        for t in range(D // 128):
            out_ref[pl.ds(i * PACK + t * OWN, OWN), :] = sums[
                i * OWN : (i + 1) * OWN, t * 128 : (t + 1) * 128
            ].astype(BF16)
        tail = jnp.zeros((16, 128), F32)
        for q, v in enumerate((high, low)):
            for h in range(2):
                at = i * OWN + h * 16
                tail = jnp.where(lane == 2 * q + h, v[at : at + 16], tail)
        out_ref[pl.ds(i * PACK + PACK - 16, 16), :] = tail.astype(BF16)


def sums_of(lses, ps, ms, embs, last):
    n = len(PARTS)
    return pl.pallas_call(
        functools.partial(sum_kernel, last),
        out_shape=(pltpu.VMEM((Z * PACK, 128), BF16), *([pltpu.VMEM((8, 128), F32)] if last else [])),
        in_specs=[VMEM] * (1 + 3 * n),
        out_specs=(VMEM,) * (1 + last),
        scratch_shapes=[pltpu.VMEM((X * 8, 128), F32)],
        compiler_params=limit(16),
        name="sums",
    )(lses, *ps, *ms, *embs)


def update_kernel(last, got_ref, cur_ref, *refs):
    if last:
        lse_ref, new_ref, out_ref, row_ref = refs
        row_ref[...] = lse_ref[...]
    else:
        new_ref, out_ref = refs

    def total(at, n):
        return sum(got_ref[pl.ds(i * PACK + at, n), :].astype(F32) for i in range(Z))

    tail = total(PACK - 16, 16)
    tail = tail[:, :2] + tail[:, 2:4]
    counts = jnp.concatenate([tail[:, :1], tail[:, 1:]], axis=0)
    for t in range(D // 128):
        lanes = slice(t * 128, (t + 1) * 128)
        new = (total(t * OWN, OWN) + cur_ref[:, lanes]) / (counts + 1.0)
        new_ref[:, lanes] = new
        if not last:
            for i in range(Z):
                out_ref[pl.ds(i * OWN, OWN), lanes] = new.astype(BF16)
    if last:
        row = lax.broadcasted_iota(jnp.int32, (OWN, OWN), 0)
        lane = lax.broadcasted_iota(jnp.int32, (OWN, OWN), 1)
        out_ref[...] = jnp.sum(jnp.where(row == lane, counts, 0.0), axis=0, keepdims=True)


def update(got, current, row_lse=None):
    last = row_lse is not None
    return pl.pallas_call(
        functools.partial(update_kernel, last),
        out_shape=(
            (shape(OWN, D), shape(1, OWN), shape(8, 128)) if last else (shape(OWN, D), shape(K, D, dtype=BF16))
        ),
        in_specs=[VMEM] * (2 + last),
        out_specs=(VMEM,) * (2 + last),
        compiler_params=limit(8),
        name="update",
    )(got, current, *([row_lse] if last else []))


def shift(v, axis, size, k):
    return lax.ppermute(v, axis, [(i, (i + k) % size) for i in range(size)])


def swap(v):
    return shift(v, "c", C, 1)


def exchange(v, axes, orders):
    groups = [[C * i + c for i in orders[c]] for c in range(C)]
    return lax.all_to_all(v, (*axes, "c"), 0, 0, axis_index_groups=groups, tiled=True)


def on_device(embeddings, centroids):
    far = shift(quarter_of(embeddings), "x", X, 2)
    mine, copies = prepare(embeddings, centroids)
    left, right = shift(mine, "x", X, 1), shift(mine, "x", X, 3)
    quarters = [shift(far, "y", Y, k) for k in range(1, Y)]
    copies, far = lax.optimization_barrier((copies, far))
    cent = exchange(copies, ("z",), RING)
    own = arrive(cent, PARTS[0], (embeddings,))
    left, right, quarters, first = lax.optimization_barrier((left, right, quarters, own[3]))
    far = join((far, *quarters))
    near = arrive(cent, PARTS[1], (left, swap(left), right, swap(right)))
    far = arrive(cent, PARTS[2], (far, swap(far)), (first, near[3]))
    embs, ps, ms, (_, _, lse) = zip(own, near, far)
    current = centroids
    for step in range(ITERS):
        if step > 0:
            cent = exchange(out, ("z",), RING)
            ps, ms, lse = score(cent, embs)
        lses = exchange(combine(lse, swap(lse)), ("x", "y"), PLANE)
        last = step == ITERS - 1
        sums, *row_lse = sums_of(lses, ps, ms, embs, last)
        got = exchange(sums, ("z",), RING)
        if not last:
            current, out = update(got, current)
    current, counts, row_lse = update(got, current, row_lse[0])
    return current, counts.reshape(OWN), row_lse.reshape(COL)


def solution(mesh):
    split = Mesh(mesh.devices.reshape(Z, X, Y, C), ("z", "x", "y", "c"))
    dp, every = ("z", "x"), ("z", "x", "y", "c")
    return jax.shard_map(
        on_device,
        mesh=split,
        in_specs=(P(dp, None), P(every, None)),
        out_specs=(P(every, None), P(every), P(dp)),
        check_vma=False,
    )
```

```python
import functools
import math

import jax
import jax.numpy as jnp
from jax import lax
from jax.experimental import pallas as pl
from jax.experimental.pallas import tpu as pltpu
from jax.sharding import Mesh
from jax.sharding import PartitionSpec as P

ITERS = 2
D = 768
Z, X, Y, C = 8, 4, 4, 2
OWN = 32
K = Z * OWN
COL = 1024
HALF = COL // 2
QUARTER = HALF // Y
PACK = OWN * D // 128 + 16
F32, BF16 = jnp.float32, jnp.bfloat16
SCALE = 50.0 * math.log2(math.e)
VMEM = pl.BlockSpec(memory_space=pltpu.VMEM)
ANY = pl.BlockSpec(memory_space=pl.ANY)
RING = ((0, 4, 2, 6, 1, 5, 3, 7), (7, 3, 5, 1, 6, 2, 4, 0))
PLANE = (tuple(range(X * Y)), tuple(range(X * Y))[::-1])
PARTS = ((0,), (1, 3), (2,))
ROWS = tuple(COL * len(part) for part in PARTS)


def in_hbm(v):
    return pltpu.with_memory_space_constraint(v, pltpu.HBM)


def limit(mib):
    return pltpu.CompilerParams(vmem_limit_bytes=mib << 20)


def shape(*dims, dtype=F32):
    return jax.ShapeDtypeStruct(dims, dtype)


def rows_to_tile(v):
    return jnp.concatenate([v[:, i * 128 : (i + 1) * 128] for i in range(v.shape[1] // 128)], axis=0)


def tile_to_rows(v):
    return jnp.concatenate([v[i : i + 1] for i in range(v.shape[0])], axis=1)


def column_of(k):
    return pl.ds(pl.multiple_of(8 * lax.rem(lax.axis_index("x") + (X - k), X), 8), 8)


def quarter_kernel(emb_ref, quarter_ref, sems):
    at = lax.axis_index("c") * HALF + lax.axis_index("y") * QUARTER
    waits = []
    for i in range(0, QUARTER, 32):
        rows = pl.ds(pl.multiple_of(at + i, 32), 32)
        waits.append(pltpu.make_async_copy(emb_ref.at[rows], quarter_ref.at[pl.ds(i, 32)], sems.at[i // 32]))
        waits[-1].start()
    for wait in waits:
        wait.wait()


def quarter_of(emb):
    return pl.pallas_call(
        quarter_kernel,
        out_shape=pltpu.VMEM((QUARTER, D), BF16),
        in_specs=[ANY],
        out_specs=VMEM,
        scratch_shapes=[pltpu.SemaphoreType.DMA((QUARTER // 32,))],
        compiler_params=limit(4),
        name="quarter",
    )(in_hbm(emb))


def prepare_kernel(emb_ref, cent_ref, mine_ref, copies_ref, mine, cent, copies, sems, out_sems, cent_sem, copies_sem):
    read = pltpu.make_async_copy(cent_ref, cent, cent_sem)
    read.start()
    at = pl.multiple_of(lax.axis_index("c") * HALF, HALF)
    reads, writes = [], []
    for i in range(HALF // 64):
        rows = pl.ds(i * 64, 64)
        reads.append(pltpu.make_async_copy(emb_ref.at[pl.ds(at + i * 64, 64)], mine.at[rows], sems.at[i]))
        writes.append(pltpu.make_async_copy(mine.at[rows], mine_ref.at[rows], out_sems.at[i]))
        reads[-1].start()
    read.wait()
    for i in range(Z):
        copies[pl.ds(i * OWN, OWN), :] = cent[...].astype(BF16)
    writes.append(pltpu.make_async_copy(copies, copies_ref, copies_sem))
    writes[-1].start()
    for i in range(HALF // 64):
        reads[i].wait()
        writes[i].start()
    for write in writes:
        write.wait()


def prepare(emb, cent):
    return pl.pallas_call(
        prepare_kernel,
        out_shape=(pltpu.HBM((HALF, D), BF16), pltpu.HBM((K, D), BF16)),
        in_specs=[ANY, ANY],
        out_specs=(ANY,) * 2,
        scratch_shapes=[
            pltpu.VMEM((HALF, D), BF16),
            pltpu.VMEM((OWN, D), F32),
            pltpu.VMEM((K, D), BF16),
            pltpu.SemaphoreType.DMA((HALF // 64,)),
            pltpu.SemaphoreType.DMA((HALF // 64,)),
            pltpu.SemaphoreType.DMA,
            pltpu.SemaphoreType.DMA,
        ],
        compiler_params=limit(4),
        name="prepare",
    )(in_hbm(emb), in_hbm(cent))


def join_kernel(*refs):
    y = lax.axis_index("y")
    for i, ref in enumerate(refs[:-1]):
        at = pl.multiple_of(QUARTER * lax.rem(y + (Y - i), Y), QUARTER)
        refs[-1][pl.ds(at, QUARTER), :] = ref[...]


def join(quarters):
    return pl.pallas_call(
        join_kernel,
        out_shape=pltpu.VMEM((HALF, D), BF16),
        in_specs=[VMEM] * Y,
        out_specs=VMEM,
        compiler_params=limit(4),
        name="join",
    )(*quarters)


def score_rows(cent, half_squares, emb, p_ref, m_ref):
    dots = lax.dot_general(cent, emb, (((1,), (1,)), ((), ())), preferred_element_type=F32)
    logits = dots * SCALE - half_squares
    peak = jnp.max(logits, axis=0, keepdims=True)
    p = jnp.exp2(logits - peak)
    total = jnp.sum(p, axis=0, keepdims=True)
    p_ref[...] = p.astype(BF16)
    m_ref[...] = rows_to_tile(peak)
    return rows_to_tile(peak + jnp.log2(total))


def half_squares_of(cent):
    wide = cent.astype(F32)
    return (0.5 * SCALE) * jnp.sum(wide * wide, axis=1, keepdims=True)


def spread(part, lse, lse_ref):
    for j, k in enumerate(part):
        lse_ref[column_of(k), :] = lse[8 * j : 8 * j + 8]


def arrive_kernel(part, before, cent_ref, *refs):
    emb, p_ref, m_ref, l_ref = refs[-4:]
    pieces = refs[: len(refs) - 4 - before]
    earlier = refs[len(pieces) : -4]
    c = lax.axis_index("c")
    cent = cent_ref[...].astype(BF16)
    half_squares = half_squares_of(cent)
    if part == (0,):
        emb[...] = pieces[0][...]
    else:
        size = pieces[0].shape[0]
        n = HALF // size
        for i, piece in enumerate(pieces):
            half = c if i // n % 2 == 0 else 1 - c
            at = pl.multiple_of(i // (2 * n) * COL + half * HALF + i % n * size, size)
            emb[pl.ds(at, size), :] = piece[...]
    lse = score_rows(cent, half_squares, emb[...], p_ref, m_ref)
    if before:
        spread(part, lse, l_ref)
        for other, ref in zip(PARTS, earlier):
            spread(other, ref[...], l_ref)
    else:
        l_ref[...] = lse


def arrive(cent, part, pieces, earlier=()):
    rows = COL * len(part)
    return pl.pallas_call(
        functools.partial(arrive_kernel, part, len(earlier)),
        out_shape=(
            pltpu.VMEM((rows, D), BF16),
            pltpu.VMEM((K, rows), BF16),
            pltpu.VMEM((rows // 128, 128), F32),
            pltpu.VMEM((X * 8 if earlier else rows // 128, 128), F32),
        ),
        in_specs=[VMEM] * (1 + len(pieces) + len(earlier)),
        out_specs=(VMEM,) * 4,
        compiler_params=limit(16),
        name="arrive",
    )(cent, *pieces, *earlier)


def score_kernel(cent_ref, *refs):
    n = len(PARTS)
    embs, ps, ms, l_ref = refs[:n], refs[n : 2 * n], refs[2 * n : 3 * n], refs[3 * n]
    cent = cent_ref[...]
    half_squares = half_squares_of(cent)
    for part, emb, p_ref, m_ref in zip(PARTS, embs, ps, ms):
        spread(part, score_rows(cent, half_squares, emb[...], p_ref, m_ref), l_ref)


def score(cent, embs):
    n = len(PARTS)
    outs = pl.pallas_call(
        score_kernel,
        out_shape=(
            *(pltpu.VMEM((K, r), BF16) for r in ROWS),
            *(pltpu.VMEM((r // 128, 128), F32) for r in ROWS),
            pltpu.VMEM((X * 8, 128), F32),
        ),
        in_specs=[VMEM] * (1 + n),
        out_specs=(VMEM,) * (2 * n + 1),
        compiler_params=limit(16),
        name="score",
    )(cent, *embs)
    return outs[:n], outs[n : 2 * n], outs[2 * n]


def combine_kernel(a_ref, b_ref, out_ref):
    a, b = a_ref[...], b_ref[...]
    peak = jnp.maximum(a, b)
    both = peak + jnp.log2(jnp.exp2(a - peak) + jnp.exp2(b - peak))
    for i in range(X * Y):
        out_ref[pl.ds(i * 32, 32), :] = both


def combine(a, b):
    return pl.pallas_call(
        combine_kernel,
        out_shape=pltpu.VMEM((X * Y * 32, 128), F32),
        in_specs=[VMEM] * 2,
        out_specs=VMEM,
        compiler_params=limit(2),
        name="combine",
    )(a, b)


def sum_kernel(last, lses_ref, *refs):
    n = len(PARTS)
    ps, ms, embs = refs[:n], refs[n : 2 * n], refs[2 * n : 3 * n]
    out_ref, lse_ref = refs[3 * n], refs[-1]
    lses = [lses_ref[pl.ds(i * 32, 32), :] for i in range(X * Y)]
    peak = functools.reduce(jnp.maximum, lses)
    total = sum(jnp.exp2(v - peak) for v in lses)
    lse_ref[...] = peak + jnp.log2(total)
    if last:
        refs[3 * n + 1][...] = lse_ref[column_of(0), :] * math.log(2.0)
    weights = jnp.zeros((K, 128), F32)
    sums = jnp.zeros((K, D), F32)
    for part, p_ref, m_ref, emb in zip(PARTS, ps, ms, embs):
        resps = []
        for j, k in enumerate(part):
            factor = tile_to_rows(jnp.exp2(m_ref[pl.ds(j * 8, 8), :] - lse_ref[column_of(k), :]))
            resp = (p_ref[:, pl.ds(j * COL, COL)].astype(F32) * factor).astype(BF16)
            wide = resp.astype(F32)
            for i in range(COL // 128):
                weights += wide[:, i * 128 : (i + 1) * 128]
            resps.append(resp)
        sums += jnp.dot(jnp.concatenate(resps, axis=1), emb[...], preferred_element_type=F32)
    counts = jnp.sum(weights, axis=1, keepdims=True)
    high = counts.astype(BF16).astype(F32)
    low = counts - high
    lane = lax.broadcasted_iota(jnp.int32, (16, 128), 1)
    for i in range(Z):
        for t in range(D // 128):
            out_ref[pl.ds(i * PACK + t * OWN, OWN), :] = sums[
                i * OWN : (i + 1) * OWN, t * 128 : (t + 1) * 128
            ].astype(BF16)
        tail = jnp.zeros((16, 128), F32)
        for q, v in enumerate((high, low)):
            for h in range(2):
                at = i * OWN + h * 16
                tail = jnp.where(lane == 2 * q + h, v[at : at + 16], tail)
        out_ref[pl.ds(i * PACK + PACK - 16, 16), :] = tail.astype(BF16)


def sums_of(lses, ps, ms, embs, last):
    n = len(PARTS)
    return pl.pallas_call(
        functools.partial(sum_kernel, last),
        out_shape=(pltpu.VMEM((Z * PACK, 128), BF16), *([pltpu.VMEM((8, 128), F32)] if last else [])),
        in_specs=[VMEM] * (1 + 3 * n),
        out_specs=(VMEM,) * (1 + last),
        scratch_shapes=[pltpu.VMEM((X * 8, 128), F32)],
        compiler_params=limit(16),
        name="sums",
    )(lses, *ps, *ms, *embs)


def update_kernel(last, got_ref, cur_ref, *refs):
    if last:
        lse_ref, new_ref, out_ref, row_ref = refs
        row_ref[...] = lse_ref[...]
    else:
        new_ref, out_ref = refs

    def total(at, n):
        return sum(got_ref[pl.ds(i * PACK + at, n), :].astype(F32) for i in range(Z))

    tail = total(PACK - 16, 16)
    tail = tail[:, :2] + tail[:, 2:4]
    counts = jnp.concatenate([tail[:, :1], tail[:, 1:]], axis=0)
    for t in range(D // 128):
        lanes = slice(t * 128, (t + 1) * 128)
        new = (total(t * OWN, OWN) + cur_ref[:, lanes]) / (counts + 1.0)
        new_ref[:, lanes] = new
        if not last:
            for i in range(Z):
                out_ref[pl.ds(i * OWN, OWN), lanes] = new.astype(BF16)
    if last:
        row = lax.broadcasted_iota(jnp.int32, (OWN, OWN), 0)
        lane = lax.broadcasted_iota(jnp.int32, (OWN, OWN), 1)
        out_ref[...] = jnp.sum(jnp.where(row == lane, counts, 0.0), axis=0, keepdims=True)


def update(got, current, row_lse=None):
    last = row_lse is not None
    return pl.pallas_call(
        functools.partial(update_kernel, last),
        out_shape=(
            (shape(OWN, D), shape(1, OWN), shape(8, 128)) if last else (shape(OWN, D), shape(K, D, dtype=BF16))
        ),
        in_specs=[VMEM] * (2 + last),
        out_specs=(VMEM,) * (2 + last),
        compiler_params=limit(8),
        name="update",
    )(got, current, *([row_lse] if last else []))


def shift(v, axis, size, k):
    return lax.ppermute(v, axis, [(i, (i + k) % size) for i in range(size)])


def swap(v):
    return shift(v, "c", C, 1)


def exchange(v, axes, orders):
    groups = [[C * i + c for i in orders[c]] for c in range(C)]
    return lax.all_to_all(v, (*axes, "c"), 0, 0, axis_index_groups=groups, tiled=True)


def on_device(embeddings, centroids):
    far = shift(quarter_of(embeddings), "x", X, 2)
    mine, copies = prepare(embeddings, centroids)
    left, right = shift(mine, "x", X, 1), shift(mine, "x", X, 3)
    quarters = {k: shift(far, "y", Y, k) for k in (2, 1, 3)}
    quarters = [quarters[k] for k in range(1, Y)]
    copies, far = lax.optimization_barrier((copies, far))
    cent = exchange(copies, ("z",), RING)
    own = arrive(cent, PARTS[0], (embeddings,))
    left, right, quarters, first = lax.optimization_barrier((left, right, quarters, own[3]))
    far = join((far, *quarters))
    near = arrive(cent, PARTS[1], (left, swap(left), right, swap(right)))
    far = arrive(cent, PARTS[2], (far, swap(far)), (first, near[3]))
    embs, ps, ms, (_, _, lse) = zip(own, near, far)
    current = centroids
    for step in range(ITERS):
        if step > 0:
            cent = exchange(out, ("z",), RING)
            ps, ms, lse = score(cent, embs)
        lses = exchange(combine(lse, swap(lse)), ("x", "y"), PLANE)
        last = step == ITERS - 1
        sums, *row_lse = sums_of(lses, ps, ms, embs, last)
        got = exchange(sums, ("z",), RING)
        if not last:
            current, out = update(got, current)
    current, counts, row_lse = update(got, current, row_lse[0])
    return current, counts.reshape(OWN), row_lse.reshape(COL)


def solution(mesh):
    split = Mesh(mesh.devices.reshape(Z, X, Y, C), ("z", "x", "y", "c"))
    dp, every = ("z", "x"), ("z", "x", "y", "c")
    return jax.shard_map(
        on_device,
        mesh=split,
        in_specs=(P(dp, None), P(every, None)),
        out_specs=(P(every, None), P(every), P(dp)),
        check_vma=False,
    )
```

```python
import functools
import math

import jax
import jax.numpy as jnp
from jax import lax
from jax.experimental import pallas as pl
from jax.experimental.pallas import tpu as pltpu
from jax.sharding import Mesh
from jax.sharding import PartitionSpec as P

ITERS = 2
D = 768
Z, X, Y, C = 8, 4, 4, 2
OWN = 32
K = Z * OWN
COL = 1024
HALF = COL // 2
QUARTER = HALF // Y
PACK = OWN * D // 128 + 16
F32, BF16 = jnp.float32, jnp.bfloat16
SCALE = 50.0 * math.log2(math.e)
VMEM = pl.BlockSpec(memory_space=pltpu.VMEM)
ANY = pl.BlockSpec(memory_space=pl.ANY)
RING = (tuple(range(Z))[::-1], tuple(range(Z))[::-1])
PLANE = (tuple(range(X * Y)), tuple(range(X * Y))[::-1])
PARTS = ((0,), (1, 3), (2,))
ROWS = tuple(COL * len(part) for part in PARTS)


def in_hbm(v):
    return pltpu.with_memory_space_constraint(v, pltpu.HBM)


def limit(mib):
    return pltpu.CompilerParams(vmem_limit_bytes=mib << 20)


def shape(*dims, dtype=F32):
    return jax.ShapeDtypeStruct(dims, dtype)


def rows_to_tile(v):
    return jnp.concatenate([v[:, i * 128 : (i + 1) * 128] for i in range(v.shape[1] // 128)], axis=0)


def tile_to_rows(v):
    return jnp.concatenate([v[i : i + 1] for i in range(v.shape[0])], axis=1)


def column_of(k):
    return pl.ds(pl.multiple_of(8 * lax.rem(lax.axis_index("x") + (X - k), X), 8), 8)


def quarter_kernel(emb_ref, quarter_ref, sems):
    at = lax.axis_index("c") * HALF + lax.axis_index("y") * QUARTER
    waits = []
    for i in range(0, QUARTER, 32):
        rows = pl.ds(pl.multiple_of(at + i, 32), 32)
        waits.append(pltpu.make_async_copy(emb_ref.at[rows], quarter_ref.at[pl.ds(i, 32)], sems.at[i // 32]))
        waits[-1].start()
    for wait in waits:
        wait.wait()


def quarter_of(emb):
    return pl.pallas_call(
        quarter_kernel,
        out_shape=pltpu.VMEM((QUARTER, D), BF16),
        in_specs=[ANY],
        out_specs=VMEM,
        scratch_shapes=[pltpu.SemaphoreType.DMA((QUARTER // 32,))],
        compiler_params=limit(4),
        name="quarter",
    )(in_hbm(emb))


def prepare_kernel(emb_ref, cent_ref, mine_ref, copies_ref, mine, cent, copies, sems, out_sems, cent_sem, copies_sem):
    read = pltpu.make_async_copy(cent_ref, cent, cent_sem)
    read.start()
    at = pl.multiple_of(lax.axis_index("c") * HALF, HALF)
    reads, writes = [], []
    for i in range(HALF // 64):
        rows = pl.ds(i * 64, 64)
        reads.append(pltpu.make_async_copy(emb_ref.at[pl.ds(at + i * 64, 64)], mine.at[rows], sems.at[i]))
        writes.append(pltpu.make_async_copy(mine.at[rows], mine_ref.at[rows], out_sems.at[i]))
        reads[-1].start()
    read.wait()
    for i in range(Z):
        copies[pl.ds(i * OWN, OWN), :] = cent[...].astype(BF16)
    writes.append(pltpu.make_async_copy(copies, copies_ref, copies_sem))
    writes[-1].start()
    for i in range(HALF // 64):
        reads[i].wait()
        writes[i].start()
    for write in writes:
        write.wait()


def prepare(emb, cent):
    return pl.pallas_call(
        prepare_kernel,
        out_shape=(pltpu.HBM((HALF, D), BF16), pltpu.HBM((K, D), BF16)),
        in_specs=[ANY, ANY],
        out_specs=(ANY,) * 2,
        scratch_shapes=[
            pltpu.VMEM((HALF, D), BF16),
            pltpu.VMEM((OWN, D), F32),
            pltpu.VMEM((K, D), BF16),
            pltpu.SemaphoreType.DMA((HALF // 64,)),
            pltpu.SemaphoreType.DMA((HALF // 64,)),
            pltpu.SemaphoreType.DMA,
            pltpu.SemaphoreType.DMA,
        ],
        compiler_params=limit(4),
        name="prepare",
    )(in_hbm(emb), in_hbm(cent))


def join_kernel(*refs):
    y = lax.axis_index("y")
    for i, ref in enumerate(refs[:-1]):
        at = pl.multiple_of(QUARTER * lax.rem(y + (Y - i), Y), QUARTER)
        refs[-1][pl.ds(at, QUARTER), :] = ref[...]


def join(quarters):
    return pl.pallas_call(
        join_kernel,
        out_shape=pltpu.VMEM((HALF, D), BF16),
        in_specs=[VMEM] * Y,
        out_specs=VMEM,
        compiler_params=limit(4),
        name="join",
    )(*quarters)


def score_rows(cent, half_squares, emb, p_ref, m_ref):
    dots = lax.dot_general(cent, emb, (((1,), (1,)), ((), ())), preferred_element_type=F32)
    logits = dots * SCALE - half_squares
    peak = jnp.max(logits, axis=0, keepdims=True)
    p = jnp.exp2(logits - peak)
    total = jnp.sum(p, axis=0, keepdims=True)
    p_ref[...] = p.astype(BF16)
    m_ref[...] = rows_to_tile(peak)
    return rows_to_tile(peak + jnp.log2(total))


def half_squares_of(cent):
    wide = cent.astype(F32)
    return (0.5 * SCALE) * jnp.sum(wide * wide, axis=1, keepdims=True)


def spread(part, lse, lse_ref):
    for j, k in enumerate(part):
        lse_ref[column_of(k), :] = lse[8 * j : 8 * j + 8]


def arrive_kernel(part, before, cent_ref, *refs):
    emb, p_ref, m_ref, l_ref = refs[-4:]
    pieces = refs[: len(refs) - 4 - before]
    earlier = refs[len(pieces) : -4]
    c = lax.axis_index("c")
    cent = cent_ref[...].astype(BF16)
    half_squares = half_squares_of(cent)
    if part == (0,):
        emb[...] = pieces[0][...]
    else:
        size = pieces[0].shape[0]
        n = HALF // size
        for i, piece in enumerate(pieces):
            half = c if i // n % 2 == 0 else 1 - c
            at = pl.multiple_of(i // (2 * n) * COL + half * HALF + i % n * size, size)
            emb[pl.ds(at, size), :] = piece[...]
    lse = score_rows(cent, half_squares, emb[...], p_ref, m_ref)
    if before:
        spread(part, lse, l_ref)
        for other, ref in zip(PARTS, earlier):
            spread(other, ref[...], l_ref)
    else:
        l_ref[...] = lse


def arrive(cent, part, pieces, earlier=()):
    rows = COL * len(part)
    return pl.pallas_call(
        functools.partial(arrive_kernel, part, len(earlier)),
        out_shape=(
            pltpu.VMEM((rows, D), BF16),
            pltpu.VMEM((K, rows), BF16),
            pltpu.VMEM((rows // 128, 128), F32),
            pltpu.VMEM((X * 8 if earlier else rows // 128, 128), F32),
        ),
        in_specs=[VMEM] * (1 + len(pieces) + len(earlier)),
        out_specs=(VMEM,) * 4,
        compiler_params=limit(16),
        name="arrive",
    )(cent, *pieces, *earlier)


def score_kernel(cent_ref, *refs):
    n = len(PARTS)
    embs, ps, ms, l_ref = refs[:n], refs[n : 2 * n], refs[2 * n : 3 * n], refs[3 * n]
    cent = cent_ref[...]
    half_squares = half_squares_of(cent)
    for part, emb, p_ref, m_ref in zip(PARTS, embs, ps, ms):
        spread(part, score_rows(cent, half_squares, emb[...], p_ref, m_ref), l_ref)


def score(cent, embs):
    n = len(PARTS)
    outs = pl.pallas_call(
        score_kernel,
        out_shape=(
            *(pltpu.VMEM((K, r), BF16) for r in ROWS),
            *(pltpu.VMEM((r // 128, 128), F32) for r in ROWS),
            pltpu.VMEM((X * 8, 128), F32),
        ),
        in_specs=[VMEM] * (1 + n),
        out_specs=(VMEM,) * (2 * n + 1),
        compiler_params=limit(16),
        name="score",
    )(cent, *embs)
    return outs[:n], outs[n : 2 * n], outs[2 * n]


def combine_kernel(a_ref, b_ref, out_ref):
    a, b = a_ref[...], b_ref[...]
    peak = jnp.maximum(a, b)
    both = peak + jnp.log2(jnp.exp2(a - peak) + jnp.exp2(b - peak))
    for i in range(X * Y):
        out_ref[pl.ds(i * 32, 32), :] = both


def combine(a, b):
    return pl.pallas_call(
        combine_kernel,
        out_shape=pltpu.VMEM((X * Y * 32, 128), F32),
        in_specs=[VMEM] * 2,
        out_specs=VMEM,
        compiler_params=limit(2),
        name="combine",
    )(a, b)


def sum_kernel(last, lses_ref, *refs):
    n = len(PARTS)
    ps, ms, embs = refs[:n], refs[n : 2 * n], refs[2 * n : 3 * n]
    out_ref, lse_ref = refs[3 * n], refs[-1]
    lses = [lses_ref[pl.ds(i * 32, 32), :] for i in range(X * Y)]
    peak = functools.reduce(jnp.maximum, lses)
    total = sum(jnp.exp2(v - peak) for v in lses)
    lse_ref[...] = peak + jnp.log2(total)
    if last:
        refs[3 * n + 1][...] = lse_ref[column_of(0), :] * math.log(2.0)
    weights = jnp.zeros((K, 128), F32)
    sums = jnp.zeros((K, D), F32)
    for part, p_ref, m_ref, emb in zip(PARTS, ps, ms, embs):
        resps = []
        for j, k in enumerate(part):
            factor = tile_to_rows(jnp.exp2(m_ref[pl.ds(j * 8, 8), :] - lse_ref[column_of(k), :]))
            resp = (p_ref[:, pl.ds(j * COL, COL)].astype(F32) * factor).astype(BF16)
            wide = resp.astype(F32)
            for i in range(COL // 128):
                weights += wide[:, i * 128 : (i + 1) * 128]
            resps.append(resp)
        sums += jnp.dot(jnp.concatenate(resps, axis=1), emb[...], preferred_element_type=F32)
    counts = jnp.sum(weights, axis=1, keepdims=True)
    high = counts.astype(BF16).astype(F32)
    low = counts - high
    lane = lax.broadcasted_iota(jnp.int32, (16, 128), 1)
    for i in range(Z):
        for t in range(D // 128):
            out_ref[pl.ds(i * PACK + t * OWN, OWN), :] = sums[
                i * OWN : (i + 1) * OWN, t * 128 : (t + 1) * 128
            ].astype(BF16)
        tail = jnp.zeros((16, 128), F32)
        for q, v in enumerate((high, low)):
            for h in range(2):
                at = i * OWN + h * 16
                tail = jnp.where(lane == 2 * q + h, v[at : at + 16], tail)
        out_ref[pl.ds(i * PACK + PACK - 16, 16), :] = tail.astype(BF16)


def sums_of(lses, ps, ms, embs, last):
    n = len(PARTS)
    return pl.pallas_call(
        functools.partial(sum_kernel, last),
        out_shape=(pltpu.VMEM((Z * PACK, 128), BF16), *([pltpu.VMEM((8, 128), F32)] if last else [])),
        in_specs=[VMEM] * (1 + 3 * n),
        out_specs=(VMEM,) * (1 + last),
        scratch_shapes=[pltpu.VMEM((X * 8, 128), F32)],
        compiler_params=limit(16),
        name="sums",
    )(lses, *ps, *ms, *embs)


def update_kernel(last, got_ref, cur_ref, *refs):
    if last:
        lse_ref, new_ref, out_ref, row_ref = refs
        row_ref[...] = lse_ref[...]
    else:
        new_ref, out_ref = refs

    def total(at, n):
        return sum(got_ref[pl.ds(i * PACK + at, n), :].astype(F32) for i in range(Z))

    tail = total(PACK - 16, 16)
    tail = tail[:, :2] + tail[:, 2:4]
    counts = jnp.concatenate([tail[:, :1], tail[:, 1:]], axis=0)
    for t in range(D // 128):
        lanes = slice(t * 128, (t + 1) * 128)
        new = (total(t * OWN, OWN) + cur_ref[:, lanes]) / (counts + 1.0)
        new_ref[:, lanes] = new
        if not last:
            for i in range(Z):
                out_ref[pl.ds(i * OWN, OWN), lanes] = new.astype(BF16)
    if last:
        row = lax.broadcasted_iota(jnp.int32, (OWN, OWN), 0)
        lane = lax.broadcasted_iota(jnp.int32, (OWN, OWN), 1)
        out_ref[...] = jnp.sum(jnp.where(row == lane, counts, 0.0), axis=0, keepdims=True)


def update(got, current, row_lse=None):
    last = row_lse is not None
    return pl.pallas_call(
        functools.partial(update_kernel, last),
        out_shape=(
            (shape(OWN, D), shape(1, OWN), shape(8, 128)) if last else (shape(OWN, D), shape(K, D, dtype=BF16))
        ),
        in_specs=[VMEM] * (2 + last),
        out_specs=(VMEM,) * (2 + last),
        compiler_params=limit(8),
        name="update",
    )(got, current, *([row_lse] if last else []))


def shift(v, axis, size, k):
    return lax.ppermute(v, axis, [(i, (i + k) % size) for i in range(size)])


def swap(v):
    return shift(v, "c", C, 1)


def exchange(v, axes, orders):
    groups = [[C * i + c for i in orders[c]] for c in range(C)]
    return lax.all_to_all(v, (*axes, "c"), 0, 0, axis_index_groups=groups, tiled=True)


def on_device(embeddings, centroids):
    far = shift(quarter_of(embeddings), "x", X, 2)
    mine, copies = prepare(embeddings, centroids)
    left, right = shift(mine, "x", X, 1), shift(mine, "x", X, 3)
    quarters = [shift(far, "y", Y, k) for k in range(1, Y)]
    copies, far = lax.optimization_barrier((copies, far))
    cent = exchange(copies, ("z",), RING)
    own = arrive(cent, PARTS[0], (embeddings,))
    left, right, quarters, first = lax.optimization_barrier((left, right, quarters, own[3]))
    far = join((far, *quarters))
    near = arrive(cent, PARTS[1], (left, swap(left), right, swap(right)))
    far = arrive(cent, PARTS[2], (far, swap(far)), (first, near[3]))
    embs, ps, ms, (_, _, lse) = zip(own, near, far)
    current = centroids
    for step in range(ITERS):
        if step > 0:
            cent = exchange(out, ("z",), RING)
            ps, ms, lse = score(cent, embs)
        lses = exchange(combine(lse, swap(lse)), ("x", "y"), PLANE)
        last = step == ITERS - 1
        sums, *row_lse = sums_of(lses, ps, ms, embs, last)
        got = exchange(sums, ("z",), RING)
        if not last:
            current, out = update(got, current)
    current, counts, row_lse = update(got, current, row_lse[0])
    return current, counts.reshape(OWN), row_lse.reshape(COL)


def solution(mesh):
    split = Mesh(mesh.devices.reshape(Z, X, Y, C), ("z", "x", "y", "c"))
    dp, every = ("z", "x"), ("z", "x", "y", "c")
    return jax.shard_map(
        on_device,
        mesh=split,
        in_specs=(P(dp, None), P(every, None)),
        out_specs=(P(every, None), P(every), P(dp)),
        check_vma=False,
    )
```
